256 devices in a mesh: region: 8 (over z), dev: 32 (over y, x, core).
Axes of the slice: x: 4, y: 4, z: 8, core: 2. Of those that a mesh axis runs over, the one named last changes fastest.
Arguments:
- probes: float32 [512, 8, 512], P(('region', 'dev')), may hold values from -20 to 20
- coords: float32 [512, 3, 512], P(('region', 'dev')), may hold values from 0 to 1
- features: float32 [512, 16, 512], P(('region', 'dev')), may hold values from -1 to 1
- noise_var: float32 [512, 512], P(('region', 'dev')), may hold values from 0.5 to 2
- inv_scale: float32 [3], replicated, may hold values from 1.2 to 2.4
- owner_map: int32 [8, 64], P('region'), may hold values from 0 to 63, as said below
- block_pairs: int32 [8, 64, 2], P('region'), may hold values from 0 to 63, as said below
Outputs:
- solution: float32 [512, 8, 512], P(('region', 'dev'))
- residual: float32 [512, 8, 512], P(('region', 'dev'))
The draws below stay inside these ranges and needn't reach their ends.
Inputs may be any that keep to these rules, and one draw needn't show every extreme that they name: `owner_map`: each region group's row is a permutation of 0 to 63. `block_pairs`: each region group's 64 rows are pairs of two blocks of that group. With a block's device in its group taken as its slot in the group // 2, the two blocks of a pair lie on different devices, and no two listed pairs of a group join the same two devices.
All inputs are finite; a program needn't handle non-finite values.
Results may differ from the reference program's by a relative error of at most 0.00013.
Values sent between devices are 32-bit elements; how exact they have to be, the bound alone decides.
A program may use at most 64 MiB of HBM per device.

```python
import math
import jax
import jax.numpy as jnp
from jax import lax

B_DEV = 2
BLK = 512
NFEAT = 16
PROBES = 8
ITERS = 2
BR = 64
NBLK = 512
NPAIR = 64


def route_layout(key):
    region_count = NBLK // BR
    device_count = BR // B_DEV
    half_count = device_count // 2
    shift_count = half_count - 1
    regular = device_count * shift_count
    candidates = regular + half_count

    def one_region(region_key):
        owner_key, device_key, score_key, first_key, second_key = jax.random.split(region_key, 5)
        owner_slot = jax.random.permutation(owner_key, BR).astype(jnp.int32)
        device_rank = jax.random.permutation(device_key, device_count)
        hub_device = (device_rank < max(device_count // 8, 1)).astype(jnp.int32)
        base_device = jnp.concatenate([jnp.tile(jnp.arange(device_count, dtype=jnp.int32), shift_count), jnp.arange(half_count, dtype=jnp.int32)])
        shift_value = jnp.concatenate([jnp.repeat(jnp.arange(1, shift_count + 1, dtype=jnp.int32), device_count), jnp.full((half_count,), half_count, jnp.int32)])
        forced = (shift_value == half_count).astype(jnp.int32)
        other_device = (base_device + shift_value) % device_count
        touches = jnp.maximum(hub_device[base_device], hub_device[other_device])
        raw_score = jax.random.randint(score_key, (candidates,), 0, 65536)
        full_score = (raw_score + touches * 65536 + forced * 131072) * candidates + jnp.arange(candidates, dtype=jnp.int32)
        chosen = jnp.argsort(-full_score)[:NPAIR].astype(jnp.int32)
        first_local = jax.random.randint(first_key, (NPAIR,), 0, B_DEV)
        second_local = jax.random.randint(second_key, (NPAIR,), 0, B_DEV)
        first_slot = base_device[chosen] * B_DEV + first_local
        second_slot = other_device[chosen] * B_DEV + second_local
        inverse = jnp.argsort(owner_slot).astype(jnp.int32)
        listed = jnp.stack([inverse[first_slot], inverse[second_slot]], axis=1)
        return (owner_slot, listed.astype(jnp.int32))
    region_keys = jax.random.split(key, region_count)
    return jax.vmap(one_region)(region_keys)


def draw_owner_map(key, part):
    return route_layout(key)[0]


def draw_block_pairs(key, part):
    return route_layout(key)[1]


def draw_probes(key, part):
    key = jax.random.fold_in(key, 11)
    base_draw = jnp.clip(jax.random.normal(key, (NBLK, PROBES, BLK), jnp.float32), -6.0, 6.0)
    block_scale = 0.6 + 1.2 * jnp.arange(NBLK, dtype=jnp.float32).reshape(NBLK, 1, 1) / max(NBLK - 1, 1)
    return (base_draw * block_scale).astype(jnp.float32)


def draw_features(key, part):
    key = jax.random.fold_in(key, 23)
    base_level = (4.0 * math.sqrt(NBLK * BLK)) ** (-0.5)
    base_draw = jnp.clip(jax.random.normal(key, (NBLK, NFEAT, BLK), jnp.float32), -5.0, 5.0)
    block_scale = 0.6 + 1.2 * jnp.arange(NBLK, dtype=jnp.float32).reshape(NBLK, 1, 1) / max(NBLK - 1, 1)
    values = base_draw * block_scale
    return jnp.clip(values * base_level, -1.0, 1.0).astype(jnp.float32)


def shard_levels(own_key, dims, cuts, low, high):
    level = 1.0
    for position, parts in cuts:
        heights = jax.random.uniform(jax.random.fold_in(jax.random.fold_in(own_key, 6), position), (parts,), jnp.float32, low / len(cuts), high / len(cuts))
        level = level * jnp.repeat(jnp.exp(heights), dims[position] // parts).reshape((-1,) + (1,) * (len(dims) - 1 - position))
    return level


def setup_inputs(seed: int = 0) -> dict:
    keys = jax.random.split(jax.random.key(seed), 8)
    return {
        "probes": draw_probes(jax.random.fold_in(keys[7], 71), 0),
        "coords": jnp.clip(1.0 * jax.random.uniform(keys[1], (NBLK, 3, BLK), jnp.float32) ** shard_levels(keys[1], (NBLK, 3, BLK), ((0, 256),), -0.2, 0.2), 0.0, 1.0),
        "features": draw_features(jax.random.fold_in(keys[7], 71), 0),
        "noise_var": jnp.clip(jnp.exp(math.log(2.0) - 1.3862944 * jax.random.uniform(keys[3], (NBLK, BLK), jnp.float32) ** shard_levels(keys[3], (NBLK, BLK), ((0, 256),), -0.2, 0.2)), 0.5, 2.0),
        "inv_scale": jnp.clip(jnp.exp(jax.random.uniform(keys[4], (3,), jnp.float32, math.log(1.2), math.log(2.4))), 1.2, 2.4),
        "owner_map": draw_owner_map(jax.random.fold_in(keys[7], 71), 0),
        "block_pairs": draw_block_pairs(jax.random.fold_in(keys[7], 71), 0),
    }


FULL_PRECISION = lax.Precision.HIGHEST

def wendland(radius):
    inside = jnp.maximum(1.0 - radius, 0.0)
    return inside * inside * inside * inside * (4.0 * radius + 1.0)

def kernel_tile(left_points, right_points, inv_scale):
    delta_x = (left_points[0][:, None] - right_points[0][None, :]) * inv_scale[0]
    delta_y = (left_points[1][:, None] - right_points[1][None, :]) * inv_scale[1]
    delta_t = jnp.abs(left_points[2][:, None] - right_points[2][None, :]) * inv_scale[2]
    spatial = jnp.sqrt(delta_x * delta_x + delta_y * delta_y)
    return 0.25 * wendland(spatial) * wendland(delta_t)

def apply_tile(kernel_block, vectors):
    return jnp.einsum('ab,cb->ca', kernel_block, vectors, precision=FULL_PRECISION)

def apply_transposed(kernel_block, vectors):
    return jnp.einsum('ab,ca->cb', kernel_block, vectors, precision=FULL_PRECISION)

def column_sum(left_vec, right_vec):
    return lax.optimization_barrier(jnp.sum(left_vec * right_vec, axis=(0, 2)))

def reference(probes, coords, features, noise_var, inv_scale, owner_map, block_pairs):
    regions = owner_map.shape[0]
    blocks_region = owner_map.shape[1]

    def region_apply(operands):
        vectors, points, owner_slot, pair_ids = operands
        slot_pairs = owner_slot[pair_ids]
        appear = jnp.zeros((blocks_region,), jnp.float32).at[slot_pairs.reshape(-1)].add(1.0)

        def one_block(operand_set):
            block_points, block_vectors, factor = operand_set
            return factor * apply_tile(kernel_tile(block_points, block_points, inv_scale), block_vectors)
        diagonal = lax.map(one_block, (points, vectors, 1.0 + appear))

        def one_pair(running_sum, pair_slots):
            first_slot = pair_slots[0]
            second = pair_slots[1]
            kernel_block = kernel_tile(points[first_slot], points[second], inv_scale)
            running_sum = running_sum.at[first_slot].add(apply_tile(kernel_block, vectors[second]))
            running_sum = running_sum.at[second].add(apply_transposed(kernel_block, vectors[first_slot]))
            return (running_sum, None)
        coupled, unused = lax.scan(one_pair, diagonal, slot_pairs)
        return coupled

    def operate(vectors):
        coupled = lax.map(region_apply, (vectors.reshape(regions, blocks_region, vectors.shape[1], vectors.shape[2]), coords.reshape(regions, blocks_region, coords.shape[1], coords.shape[2]), owner_map, block_pairs)).reshape(vectors.shape)
        feature_load = jnp.einsum('bfn,bcn->fc', features, vectors, precision=FULL_PRECISION)
        feature_part = jnp.einsum('bfn,fc->bcn', features, feature_load, precision=FULL_PRECISION)
        return coupled + noise_var[:, None, :] * vectors + feature_part
    solution = jnp.zeros_like(probes)
    residual = probes
    direction = probes
    norm_now = column_sum(residual, residual)
    for sweep_index in range(ITERS):
        image_vec = operate(direction)
        step_size = norm_now / column_sum(direction, image_vec)
        solution = solution + step_size[None, :, None] * direction
        residual = residual - step_size[None, :, None] * image_vec
        norm_next = column_sum(residual, residual)
        direction = residual + (norm_next / norm_now)[None, :, None] * direction
        norm_now = norm_next
    return (solution, residual)
```

```python
import functools

import jax
import jax.numpy as jnp
from jax import lax
from jax.experimental import pallas as pl
from jax.experimental.pallas import tpu as pltpu
from jax.sharding import PartitionSpec as P

MESH = pl.DeviceIdType.MESH
HIGH = lax.Precision.HIGHEST
F32 = jnp.float32
BF16 = jnp.bfloat16
BLK = 512
NT = (((1,), (1,)), ((), ()))
NN = (((1,), (0,)), ((), ()))


def kernel(
    probes, coords, features, noise, inv_scale, owner_s, pairs_s, owner_v, pairs_v,
    out_sol, out_res,
    stage, sib_feat, v1, v2, v3, kh, kl, turned, quad, w2m, w3m, diag, targets, ax, ay, az, fin, fin_sib,
    s1_send, s1_recv, sib_send, sib_recv, ag_send, ag_recv, ar_send, ar_recv, fin_send, fin_recv,
):
    region = lax.axis_index("region")
    dev = lax.axis_index("dev")
    y, x, core = dev // 8, (dev // 2) % 4, dev % 2
    chip = y * 4 + x
    pos = (chip, x * 4 + y)

    def at(yy, xx, cc):
        return (region, yy * 8 + xx * 2 + cc)

    def x_peer(d, cc):
        return at(y, lax.rem(x + d, 4), cc)

    def y_peer(d, cc):
        return at(lax.rem(y + d, 4), x, cc)

    def z_peer(d):
        return (lax.rem(region + d, 8), dev)

    sibling = at(y, x, 1 - core)
    along = (x_peer, y_peer)

    barrier = pltpu.get_barrier_semaphore()
    for d in (1, 2, 3):
        for cc in (0, 1):
            pl.semaphore_signal(barrier, inc=1, device_id=x_peer(d, cc), device_id_type=MESH)
            pl.semaphore_signal(barrier, inc=1, device_id=y_peer(d, cc), device_id_type=MESH)
    pl.semaphore_signal(barrier, inc=1, device_id=sibling, device_id_type=MESH)
    for d in range(1, 8):
        pl.semaphore_signal(barrier, inc=1, device_id=z_peer(d), device_id_type=MESH)

    row = lax.broadcasted_iota(jnp.int32, (8, BLK), 0)
    low = row < 4
    for b in (0, 1):
        block = probes[b]
        for cc in (0, 1):
            stage[cc, b] = block if cc == 0 else pltpu.roll(block, 4, 0)
            stage[cc, b, 4:7, :] = coords[b]
            stage[cc, b, 7:8, :] = noise[b : b + 1, :]
        v1[b * 32 + pos[b] * 2 + core] = stage[core, b]

    pl.semaphore_wait(barrier, 20)

    def copy(src, dst, ssem, rsem, device):
        return pltpu.make_async_remote_copy(
            src_ref=src, dst_ref=dst, send_sem=ssem, recv_sem=rsem, device_id=device, device_id_type=MESH
        )

    sends = []
    feat_copy = copy(features, sib_feat, sib_send.at[2], sib_recv.at[2], sibling)
    sib_copies = []
    for b in (0, 1):
        own = v1.at[b * 32 + pos[b] * 2 + core]
        c = copy(stage.at[1 - core, b], own, sib_send.at[b], sib_recv.at[b], sibling)
        c.start()
        sib_copies.append(c)
        for d in (1, 2, 3):
            for cc in (0, 1):
                c = copy(stage.at[cc, b], own, s1_send.at[b, d - 1, cc], s1_recv.at[b, d - 1, core], along[b](d, cc))
                c.start()
                sends.append(c)
    feat_copy.start()

    def gather_copies(buf, m, stage_index, call):
        out = []
        for h in (0, 1):
            if stage_index == 0:
                span = pl.ds(h * 16 * m + pos[h] * m, m)
                peer = along[h]
            else:
                span = pl.ds(h * 16 * m + (y, x)[h] * 4 * m, 4 * m)
                peer = along[1 - h]
            for d in (1, 2, 3):
                sem = (call, stage_index, h, d - 1)
                out.append(copy(buf.at[span], buf.at[span], ag_send.at[sem], ag_recv.at[sem], peer(d, core)))
        return out

    def start_all(copies):
        for c in copies:
            c.start()
            sends.append(c)

    def arrive_all(copies):
        for c in copies:
            c.wait_recv()

    sx, sy, st = inv_scale[0], inv_scale[1], inv_scale[2]

    def make_tile(index, left, right):
        turned[...] = jnp.transpose(left)
        rx, ry, rt = right[4:5, :] * sx, right[5:6, :] * sy, right[6:7, :] * st

        def rows(i, _):
            span = pl.ds(pl.multiple_of(i * 16, 16), 16)
            part = turned[span, :]
            dx = part[:, 4:5] * sx - rx
            dy = part[:, 5:6] * sy - ry
            dt = part[:, 6:7] * st - rt
            sq = jnp.maximum(dx * dx + dy * dy, 1e-30)
            a = jnp.maximum(1.0 - sq * lax.rsqrt(sq), 0.0)
            b = jnp.maximum(1.0 - jnp.abs(dt), 0.0)
            m = a * b
            m = m * m
            m = m * m
            value = m * ((1.25 - a) * (1.25 - b))
            high = value.astype(BF16)
            kh[index, span, :] = high
            kl[index, span, :] = (value - high.astype(F32)).astype(BF16)
            return 0

        lax.fori_loop(0, 32, rows, 0, unroll=4)

    def twice(v):
        return jnp.where(low, v, pltpu.roll(v, 4, 0))

    def split(v):
        high = v.astype(BF16).astype(F32)
        return jnp.where(low, high, v - high).astype(BF16)

    def apply(v, index, dims):
        s = lax.dot_general(v, kh[index], dims, preferred_element_type=F32)
        s = s + lax.dot_general(v, kl[index], dims, preferred_element_type=F32)
        return 4.0 * (s + pltpu.roll(s, 4, 0))

    def local_slot(k):
        return (k % 2) * 32 + pos[k % 2] * 2 + k // 2

    lane64 = lax.broadcasted_iota(jnp.int32, (64, 64), 1)
    owner_row = owner_v[...].astype(F32)
    ids = pairs_v[0]
    slot_a = jnp.sum(jnp.where(ids[:, 0:1] == lane64, owner_row, 0.0), axis=1, keepdims=True)
    slot_b = jnp.sum(jnp.where(ids[:, 1:2] == lane64, owner_row, 0.0), axis=1, keepdims=True)
    first, second = [], []
    for i in range(4):
        first.append(owner_s[0, pairs_s[0, chip * 4 + i, 0]])
        second.append(owner_s[0, pairs_s[0, chip * 4 + i, 1]])

    def lane_slots(m):
        width = 2 * 16 * m * 8
        j = lax.broadcasted_iota(jnp.int32, (1, width), 1)
        n = j >> 3
        side = (j >> 2) & 1
        h = (n >= 16 * m).astype(jnp.int32)
        rest = n - h * 16 * m
        place = (rest * 171) >> 9 if m == 3 else rest >> 1
        e = rest - place * m
        q = jnp.where(h == 0, place, (place & 3) * 4 + (place >> 2))
        p = q * 4 + h * 2 + e
        pick = lax.broadcasted_iota(jnp.int32, (64, width), 0) == p
        listed = jnp.sum(jnp.where(pick, jnp.where(side == 0, slot_a, slot_b), 0.0), axis=0, keepdims=True)
        own = (q * 4 + side * 2 + h).astype(F32)
        return jnp.where(e == 2, own, listed), j & 3

    def choose(width, lanes, column, slot):
        r = lax.broadcasted_iota(jnp.int32, (8, width), 0) & 3
        hit = (lanes == slot.astype(F32)) & (r == column)
        return jnp.where(hit, 1.0, 0.0)

    lanes2, column2 = lane_slots(3)
    lanes3, column3 = lane_slots(2)
    wanted = []
    for i in range(4):
        wanted += [first[i], second[i]]
    for k in range(4):
        wanted.append(chip * 4 + k)
    for k in range(12):
        w2m[8 * k : 8 * k + 8, :] = choose(768, lanes2, column2, wanted[k])
    factor = []
    for k in range(4):
        w3m[8 * k : 8 * k + 8, :] = choose(512, lanes3, column3, wanted[8 + k])
        me = wanted[8 + k].astype(F32)
        count = jnp.where(slot_a == me, 1.0, 0.0) + jnp.where(slot_b == me, 1.0, 0.0)
        factor.append(1.0 + jnp.sum(count, axis=0, keepdims=True))

    for b in (0, 1):
        mine = stage[0, b]
        make_tile(2 * core + b, mine, mine)

    for b in (0, 1):
        sib_copies[b].wait_recv()
        for d in (1, 2, 3):
            for cc in (0, 1):
                copy(
                    stage.at[cc, b], v1.at[b * 32 + pos[b] * 2 + core], s1_send.at[b, d - 1, cc],
                    s1_recv.at[b, d - 1, cc], along[b](d, cc),
                ).wait_recv()
    second_stage = gather_copies(v1, 2, 1, 0)
    start_all(second_stage)

    feat_copy.wait_recv()
    quad[...] = jnp.zeros_like(quad)
    for k in range(4):
        here = jnp.where(core == k // 2, features[k % 2], sib_feat[k % 2])
        quad[k, 0:16, :] = here
        quad[k, 16:24, :] = v1[local_slot(k)]

    def wave(call, stage_index, buf, me, peer, count, value):
        buf[call, me] = value
        copies = []
        for d in range(1, count):
            sem = (call, stage_index, d - 1)
            copies.append(copy(buf.at[call, me], buf.at[call, me], ar_send.at[sem], ar_recv.at[sem], peer(d)))
        start_all(copies)
        return copies

    def total(call, buf, count, copies):
        arrive_all(copies)
        t = buf[call, 0]
        for i in range(1, count):
            t = t + buf[call, i]
        return t

    xp, yp = (lambda d: x_peer(d, core)), (lambda d: y_peer(d, core))

    def loads(values):
        t = jnp.zeros((8, 128), F32)
        for k in range(4):
            t = t + lax.dot_general(values(k), quad[k], NT, precision=HIGH, preferred_element_type=F32)
        return t

    wx = wave(0, 0, ax, x, xp, 4, loads(lambda k: v1[local_slot(k)]))

    for b in (0, 1):
        theirs = v1[b * 32 + pos[b] * 2 + (1 - core)]
        make_tile(2 * (1 - core) + b, theirs, theirs)
    wy = wave(0, 1, ay, y, yp, 4, total(0, ax, 4, wx))
    for k in range(4):
        mine = twice(v1[local_slot(k)])
        diag[k] = factor[k] * apply(split(mine), k, NN) + quad[k, 23:24, :] * mine
    wz = wave(0, 2, az, region, z_peer, 8, total(0, ay, 4, wy))

    arrive_all(second_stage)

    def flat(s):
        q = s >> 2
        b = s & 1
        place = jnp.where(b == 0, q, (q & 3) * 4 + (q >> 2))
        return b * 32 + place * 2 + ((s >> 1) & 1)

    for i in range(4):
        va, vb = v1[flat(first[i])], v1[flat(second[i])]
        make_tile(4 + i, va, vb)
        ya = apply(split(twice(vb)), 4 + i, NT)
        yb = apply(split(twice(va)), 4 + i, NN)
        h = i // 2
        v2[h * 48 + pos[h] * 3 + i % 2] = jnp.where(low, ya, yb)

    lane = lax.broadcasted_iota(jnp.int32, (8, 128), 1)
    row128 = lax.broadcasted_iota(jnp.int32, (8, 128), 0)
    sums1 = total(0, az, 8, wz)

    def spread(sums, k):
        g = jnp.where(lane < 16, sums, 0.0)
        return twice(lax.dot_general(g, quad[k], NN, precision=HIGH, preferred_element_type=F32))

    for b in (0, 1):
        d0 = diag[b] + spread(sums1, b)
        d1 = diag[2 + b] + spread(sums1, 2 + b)
        v2[b * 48 + pos[b] * 3 + 2] = jnp.where(low, d0, d1)

    copies = gather_copies(v2, 3, 0, 1)
    start_all(copies)
    arrive_all(copies)
    copies = gather_copies(v2, 3, 1, 1)
    start_all(copies)
    arrive_all(copies)

    def combine(weights, buf, rows):
        acc = None
        for lo_row in range(0, rows, 256):
            part = buf[lo_row // 8 : lo_row // 8 + 32].reshape(256, BLK)
            w = weights[:, lo_row : lo_row + 256].astype(BF16)
            high = part.astype(BF16)
            rest = (part - high.astype(F32)).astype(BF16)
            s = lax.dot_general(w, high, NN, preferred_element_type=F32)
            s = s + lax.dot_general(w, rest, NN, preferred_element_type=F32)
            acc = s if acc is None else acc + s
        return acc

    targets[...] = combine(w2m, v2, 768).reshape(12, 8, BLK)

    form = jnp.zeros((8, BLK), F32)
    for i in range(4):
        wa, wb = targets[2 * i], targets[2 * i + 1]
        ya = apply(split(wb), 4 + i, NT)
        yb = apply(split(wa), 4 + i, NN)
        h = i // 2
        v3[h * 32 + pos[h] * 2 + i % 2] = jnp.where(low, ya, yb)
        form = form + 2.0 * (wa * ya)
    copies3 = gather_copies(v3, 2, 0, 2)
    start_all(copies3)
    for k in range(4):
        mine = targets[8 + k]
        z = factor[k] * apply(split(mine), k, NN) + quad[k, 23:24, :] * mine
        diag[k] = z
        form = form + mine * z
        quad[k, 20:24, :] = mine[0:4, :]
    sums = loads(lambda k: targets[8 + k])
    sums = jnp.where(lane == 24, jnp.sum(form, axis=1, keepdims=True), sums)
    wx = wave(1, 0, ax, x, xp, 4, sums)
    wy = wave(1, 1, ay, y, yp, 4, total(1, ax, 4, wx))
    arrive_all(copies3)
    copies3 = gather_copies(v3, 2, 1, 2)
    start_all(copies3)
    wz = wave(1, 2, az, region, z_peer, 8, total(1, ay, 4, wy))
    arrive_all(copies3)
    coupled = combine(w3m, v3, 512).reshape(4, 8, BLK)
    sums2 = total(1, az, 8, wz)

    def entry(t, where):
        return jnp.sum(jnp.where(where, t, 0.0), axis=1, keepdims=True)

    m0 = entry(sums1, lane == 16 + row128)
    m1 = entry(sums2, lane == 16 + row128)
    m2 = entry(sums2, lane == 20 + row128)
    m3 = entry(sums2, lane == 24) + entry(sums2 * sums2, lane < 16)
    alpha = m0 / m1
    fresh = m0 - 2.0 * alpha * m1 + alpha * alpha * m2
    grow = 1.0 + fresh / m0
    curve = grow * grow * m1 - 2.0 * grow * alpha * m2 + alpha * alpha * m3
    alpha2 = fresh / curve
    ca = alpha + alpha2 * grow
    cb = alpha * alpha2
    ca = jnp.where(low, ca, pltpu.roll(jnp.broadcast_to(ca, (8, BLK)), 4, 0))
    cb = jnp.where(low, cb, pltpu.roll(jnp.broadcast_to(cb, (8, BLK)), 4, 0))
    for k in range(4):
        r0 = twice(v1[local_slot(k)])
        w1 = targets[8 + k]
        w2 = diag[k] + coupled[k] + spread(sums2, k)
        fin[k] = jnp.where(low, ca * r0 - cb * w1, r0 - ca * w1 + cb * w2)
    last = copy(fin.at[pl.ds(2 * (1 - core), 2)], fin_sib, fin_send, fin_recv, sibling)
    last.start()
    last.wait_recv()
    for b in (0, 1):
        mine, theirs = fin[2 * core + b], fin_sib[b]
        left = jnp.where(core == 0, mine, theirs)
        right = jnp.where(core == 0, theirs, mine)
        out_sol[b] = jnp.where(low, left, pltpu.roll(right, 4, 0))
        out_res[b] = jnp.where(low, pltpu.roll(left, 4, 0), right)
    for c in sends + sib_copies + [feat_copy, last]:
        c.wait_send()


def shards(probes, coords, features, noise_var, inv_scale, owner_map, block_pairs):
    vmem = pl.BlockSpec(memory_space=pltpu.VMEM)
    smem = pl.BlockSpec(memory_space=pltpu.SMEM)
    dma = pltpu.SemaphoreType.DMA
    out = jax.ShapeDtypeStruct(probes.shape, F32)
    return pl.pallas_call(
        kernel,
        out_shape=(out, out),
        in_specs=[vmem, vmem, vmem, vmem, smem, smem, smem, vmem, vmem],
        out_specs=(vmem, vmem),
        scratch_shapes=[
            pltpu.VMEM((2, 2, 8, BLK), F32),
            pltpu.VMEM((2, 16, BLK), F32),
            pltpu.VMEM((64, 8, BLK), F32),
            pltpu.VMEM((96, 8, BLK), F32),
            pltpu.VMEM((64, 8, BLK), F32),
            pltpu.VMEM((8, BLK, BLK), BF16),
            pltpu.VMEM((8, BLK, BLK), BF16),
            pltpu.VMEM((BLK, 8), F32),
            pltpu.VMEM((4, 128, BLK), F32),
            pltpu.VMEM((96, 768), F32),
            pltpu.VMEM((32, 512), F32),
            pltpu.VMEM((4, 8, BLK), F32),
            pltpu.VMEM((12, 8, BLK), F32),
            pltpu.VMEM((2, 4, 8, 128), F32),
            pltpu.VMEM((2, 4, 8, 128), F32),
            pltpu.VMEM((2, 8, 8, 128), F32),
            pltpu.VMEM((4, 8, BLK), F32),
            pltpu.VMEM((2, 8, BLK), F32),
            dma((2, 3, 2)), dma((2, 3, 2)),
            dma((3,)), dma((3,)),
            dma((3, 2, 2, 3)), dma((3, 2, 2, 3)),
            dma((2, 3, 7)), dma((2, 3, 7)),
            dma, dma,
        ],
        compiler_params=pltpu.CompilerParams(
            collective_id=0, has_side_effects=True, vmem_limit_bytes=40 << 20
        ),
        name="cg2",
    )(probes, coords, features, noise_var, inv_scale, owner_map, block_pairs, owner_map, block_pairs)


def solution(mesh):
    return jax.shard_map(
        shards,
        mesh=mesh,
        in_specs=(
            P(("region", "dev"), None, None),
            P(("region", "dev"), None, None),
            P(("region", "dev"), None, None),
            P(("region", "dev"), None),
            P(),
            P("region", None),
            P("region", None, None),
        ),
        out_specs=(P(("region", "dev"), None, None), P(("region", "dev"), None, None)),
        check_vma=False,
    )
```

```python
import jax
import jax.numpy as jnp
from jax import lax
from jax.experimental import pallas as pl
from jax.experimental.pallas import tpu as pltpu
from jax.sharding import PartitionSpec as P

MESH = pl.DeviceIdType.MESH
F32 = jnp.float32
BF16 = jnp.bfloat16
BLK = 512
NT = (((1,), (1,)), ((), ()))
NN = (((1,), (0,)), ((), ()))
PLANE = [(dy, dx) for dy in range(4) for dx in range(4) if dy or dx]


def kernel(
    probes, coords, features, noise, inv_scale, owner_s, pairs_s, owner_v, pairs_v,
    out_sol, out_res,
    points, field, halves, sib_feat, v2, dense, landed, kh, kl, turned, fh, fl, w2f, w2b, diag, targets, packed,
    sib_packed, tile, az1, ap1, az2, ap2,
    pt_send, pt_recv, pf_send, pf_recv, fd_send, fd_recv, sib_send, sib_recv, ag_send, ag_recv,
    rs_send, rs_recv, z1_send, z1_recv, p1_send, p1_recv, z2_send, z2_recv, p2_send, p2_recv,
):
    region = lax.axis_index("region")
    dev = lax.axis_index("dev")
    y, x, core = dev // 8, (dev // 2) % 4, dev % 2
    other = 1 - core
    chip = y * 4 + x
    pos = (chip, x * 4 + y)

    def plane_chip(dy, dx):
        return lax.rem(y + dy, 4) * 4 + lax.rem(x + dx, 4)

    def plane_peer(dy, dx, cc):
        return (region, plane_chip(dy, dx) * 2 + cc)

    def z_peer(d, cc):
        return (lax.rem(region + d, 8), chip * 2 + cc)

    sibling = (region, chip * 2 + other)

    barrier = pltpu.get_barrier_semaphore()
    for dy, dx in PLANE:
        pl.semaphore_signal(barrier, inc=1, device_id=plane_peer(dy, dx, core), device_id_type=MESH)
    for d in range(1, 8):
        pl.semaphore_signal(barrier, inc=1, device_id=z_peer(d, core), device_id_type=MESH)
    pl.semaphore_signal(barrier, inc=1, device_id=sibling, device_id_type=MESH)

    row = lax.broadcasted_iota(jnp.int32, (8, BLK), 0)
    low = row < 4
    lane = lax.broadcasted_iota(jnp.int32, (8, 128), 1)
    row128 = lax.broadcasted_iota(jnp.int32, (8, 128), 0)
    low128 = row128 < 4

    def flip(v):
        return pltpu.roll(v, 4, 0)

    here = core * 16 + chip
    for b in (0, 1):
        for d in range(3):
            points[here, 4 * b + d : 4 * b + d + 1, :] = coords[d, b : b + 1, :]
        points[here, 4 * b + 3 : 4 * b + 4, :] = noise[b : b + 1, :]
    p0, p1 = probes[0], probes[1]
    halves[0] = jnp.where(low, p0, flip(p1))
    halves[1] = jnp.where(low, flip(p0), p1)
    field[chip, core] = halves[core]

    pl.semaphore_wait(barrier, 23)

    sends = []

    def send(src, dst, ssem, rsem, device):
        c = pltpu.make_async_remote_copy(
            src_ref=src, dst_ref=dst, send_sem=ssem, recv_sem=rsem, device_id=device, device_id_type=MESH
        )
        c.start()
        sends.append(c)
        return c

    def arrive(copies):
        for c in copies:
            c.wait_recv()

    sib_field = send(halves.at[other], field.at[chip, core], sib_send.at[0], sib_recv.at[0], sibling)
    point_copies = []
    for n, (dy, dx) in enumerate(PLANE):
        point_copies.append(
            send(points.at[here], points.at[here], pt_send.at[n], pt_recv.at[n], plane_peer(dy, dx, core))
        )
    forwards = [send(points.at[here], points.at[here], pf_send.at[15], pf_recv.at[15], sibling)]
    sib_features = send(features, sib_feat, sib_send.at[1], sib_recv.at[1], sibling)

    sx, sy, st = inv_scale[0], inv_scale[1], inv_scale[2]

    def make_tile(index, left, right):
        turned[...] = jnp.transpose(left)
        rx, ry, rt = right[0:1, :] * sx, right[1:2, :] * sy, right[2:3, :] * st

        def rows(i, _):
            span = pl.ds(pl.multiple_of(i * 16, 16), 16)
            part = turned[span, :]
            dx = part[:, 0:1] * sx - rx
            dy = part[:, 1:2] * sy - ry
            dt = part[:, 2:3] * st - rt
            sq = jnp.maximum(dx * dx + dy * dy, 1e-30)
            a = jnp.maximum(1.0 - sq * lax.rsqrt(sq), 0.0)
            b = jnp.maximum(1.0 - jnp.abs(dt), 0.0)
            m = a * b
            m = m * m
            m = m * m
            value = m * ((1.25 - a) * (1.25 - b))
            high = value.astype(BF16)
            kh[index, span, :] = high
            kl[index, span, :] = (value - high.astype(F32)).astype(BF16)
            return 0

        lax.fori_loop(0, 32, rows, 0, unroll=4)

    def points_of(index, b):
        v = points[index]
        if isinstance(b, int):
            return v if b == 0 else flip(v)
        return jnp.where(b == 0, v, flip(v))

    def field_of(q, c, b):
        v = field[q, c]
        f = flip(v)
        first, second = jnp.where(low, v, f), jnp.where(low, f, v)
        if isinstance(b, int):
            return first if b == 0 else second
        return jnp.where(b == 0, first, second)

    def split(v):
        high = v.astype(BF16).astype(F32)
        return jnp.where(low, high, v - high).astype(BF16)

    def fold(v, high, rest, dims):
        s = lax.dot_general(v, high, dims, preferred_element_type=F32)
        s = s + lax.dot_general(v, rest, dims, preferred_element_type=F32)
        return s + flip(s)

    def apply(v, index, dims):
        return 4.0 * fold(v, kh[index], kl[index], dims)

    mine0 = points[here]
    make_tile(2 * core, mine0, mine0)

    sib_field.wait_recv()
    field_copies = []
    for n, (dy, dx) in enumerate(PLANE):
        field_copies.append(
            send(field.at[chip], field.at[chip], fd_send.at[n], fd_recv.at[n], plane_peer(dy, dx, core))
        )

    sib_features.wait_recv()

    def feature_block(k):
        return jnp.where(core == k // 2, features[k % 2], sib_feat[k % 2])

    for k in range(4):
        f = feature_block(k)
        high = f.astype(BF16)
        fh[k] = high
        fl[k] = (f - high.astype(F32)).astype(BF16)

    def loads(values):
        t = None
        for k in range(4):
            s = fold(split(values(k)), fh[k], fl[k], NT)
            t = s if t is None else t + s
        tile[:, 0:16] = t
        return tile[...]

    tile[...] = jnp.zeros_like(tile)
    az1[region] = loads(lambda k: field_of(chip, k // 2, k % 2))
    z1 = []
    for d in range(1, 8):
        z1.append(send(az1.at[region], az1.at[region], z1_send.at[d - 1], z1_recv.at[d - 1], z_peer(d, core)))

    lane64 = lax.broadcasted_iota(jnp.int32, (64, 64), 1)
    owner_row = owner_v[...].astype(F32)
    ids = jnp.transpose(pairs_v[0].astype(F32)).astype(jnp.int32)
    slot_a = jnp.sum(jnp.where(ids[:, 0:1] == lane64, owner_row, 0.0), axis=1, keepdims=True)
    slot_b = jnp.sum(jnp.where(ids[:, 1:2] == lane64, owner_row, 0.0), axis=1, keepdims=True)
    first, second = [], []
    for i in range(4):
        first.append(owner_s[0, pairs_s[0, 0, chip * 4 + i]])
        second.append(owner_s[0, pairs_s[0, 1, chip * 4 + i]])

    j = lax.broadcasted_iota(jnp.int32, (1, 768), 1)
    n = j >> 3
    side = (j >> 2) & 1
    h = (n >= 48).astype(jnp.int32)
    rest = n - h * 48
    place = (rest * 171) >> 9
    e = rest - place * 3
    q = jnp.where(h == 0, place, (place & 3) * 4 + (place >> 2))
    pick = lax.broadcasted_iota(jnp.int32, (64, 768), 0) == q * 4 + h * 2 + e
    listed = jnp.sum(jnp.where(pick, jnp.where(side == 0, slot_a, slot_b), 0.0), axis=0, keepdims=True)
    lanes2 = jnp.where(e == 2, (q * 4 + side * 2 + h).astype(F32), listed)
    same_column = (lax.broadcasted_iota(jnp.int32, (8, 768), 0) & 3) == (j & 3)
    wanted = []
    for i in range(4):
        wanted += [first[i], second[i]]
    for k in range(4):
        wanted.append(chip * 4 + k)
    for k in range(12):
        hit = (lanes2 == wanted[k].astype(F32)) & same_column
        w2f[8 * k : 8 * k + 8, :] = jnp.where(hit, 1.0, 0.0)
    w2b[...] = w2f[...].astype(BF16)
    factor = []
    for k in range(4):
        me = wanted[8 + k].astype(F32)
        count = jnp.where(slot_a == me, 1.0, 0.0) + jnp.where(slot_b == me, 1.0, 0.0)
        factor.append(1.0 + jnp.sum(count, axis=0, keepdims=True))
    lane32 = lax.broadcasted_iota(jnp.int32, (256, 32), 1)
    slot32 = jnp.zeros((256, 32), jnp.int32)
    for i in range(8):
        slot32 = jnp.where((lane32 >> 2) == i, wanted[i], slot32)
    row32 = lax.broadcasted_iota(jnp.int32, (256, 32), 0)
    w3 = jnp.where((slot32 == (row32 >> 2)) & ((lane32 & 3) == (row32 & 3)), 1.0, 0.0).astype(BF16)

    mine1 = flip(points[here])
    make_tile(2 * core + 1, mine1, mine1)

    for n, (dy, dx) in enumerate(PLANE):
        back = core * 16 + plane_chip(-dy % 4, -dx % 4)
        point_copies[n].wait_recv()
        forwards.append(send(points.at[back], points.at[back], pf_send.at[n], pf_recv.at[n], sibling))

    arrive(z1)
    t = az1[0]
    for i in range(1, 8):
        t = t + az1[i]
    ap1[chip] = t
    a1 = []
    for n, (dy, dx) in enumerate(PLANE):
        a1.append(send(ap1.at[chip], ap1.at[chip], p1_send.at[n], p1_recv.at[n], plane_peer(dy, dx, core)))

    arrive(forwards)
    for b in (0, 1):
        theirs = points_of(other * 16 + chip, b)
        make_tile(2 * other + b, theirs, theirs)

    def where_is(s):
        return s >> 2, (s >> 1) & 1, s & 1

    for i in range(4):
        qa, ca, ba = where_is(first[i])
        qb, cb, bb = where_is(second[i])
        make_tile(4 + i, points_of(ca * 16 + qa, ba), points_of(cb * 16 + qb, bb))

    def noise_of(k):
        return points[(k // 2) * 16 + chip, 4 * (k % 2) + 3 : 4 * (k % 2) + 4, :]

    for k in range(4):
        mine = field_of(chip, k // 2, k % 2)
        diag[k] = factor[k] * apply(split(mine), k, NN) + noise_of(k) * mine

    arrive(field_copies)
    for i in range(4):
        va, vb = field_of(*where_is(first[i])), field_of(*where_is(second[i]))
        ya = apply(split(vb), 4 + i, NT)
        yb = apply(split(va), 4 + i, NN)
        v2[(i // 2) * 48 + pos[i // 2] * 3 + i % 2] = jnp.where(low, ya, yb)

    arrive(a1)
    g1 = ap1[0]
    for i in range(1, 16):
        g1 = g1 + ap1[i]

    def spread(g, k):
        f = feature_block(k)
        acc = g[:, 0:1] * f[0:1, :]
        for i in range(1, 16):
            acc = acc + g[:, i : i + 1] * f[i : i + 1, :]
        return acc

    def gather_stage(stage_index):
        out = []
        for h in (0, 1):
            if stage_index == 0:
                span = pl.ds(h * 48 + pos[h] * 3, 3)
                steps = [(0, d) if h == 0 else (d, 0) for d in (1, 2, 3)]
            else:
                span = pl.ds(h * 48 + (y, x)[h] * 12, 12)
                steps = [(d, 0) if h == 0 else (0, d) for d in (1, 2, 3)]
            for d, (dy, dx) in enumerate(steps):
                sem = (stage_index, h, d)
                out.append(send(v2.at[span], v2.at[span], ag_send.at[sem], ag_recv.at[sem], plane_peer(dy, dx, core)))
        return out

    for b in (0, 1):
        d0 = diag[b] + spread(g1, b)
        d1 = diag[2 + b] + spread(g1, 2 + b)
        v2[b * 48 + pos[b] * 3 + 2] = jnp.where(low, d0, d1)
    arrive(gather_stage(0))
    arrive(gather_stage(1))

    acc = None
    for lo_row in range(0, 768, 256):
        part = v2[lo_row // 8 : lo_row // 8 + 32].reshape(256, BLK)
        w = w2b[:, lo_row : lo_row + 256]
        high = part.astype(BF16)
        less = (part - high.astype(F32)).astype(BF16)
        s = lax.dot_general(w, high, NN, preferred_element_type=F32)
        s = s + lax.dot_general(w, less, NN, preferred_element_type=F32)
        acc = s if acc is None else acc + s
    targets[...] = acc.reshape(12, 8, BLK)

    form = jnp.zeros((8, BLK), F32)
    for i in range(4):
        wa = targets[2 * i]
        ya = apply(split(targets[2 * i + 1]), 4 + i, NT)
        dense[i, 0] = ya
        form = form + 2.0 * (wa * ya)
    dot00, dot01, dot11 = jnp.zeros((8, BLK), F32), jnp.zeros((8, BLK), F32), jnp.zeros((8, BLK), F32)
    for k in range(4):
        w1 = targets[8 + k]
        r0 = field_of(chip, k // 2, k % 2)
        z = factor[k] * apply(split(w1), k, NN) + noise_of(k) * w1
        packed[k] = jnp.where(low, w1, z)
        form = form + w1 * z
        dot00 = dot00 + r0 * r0
        dot01 = dot01 + r0 * w1
        dot11 = dot11 + w1 * w1
    g2 = loads(lambda k: targets[8 + k])
    stat_a = jnp.sum(jnp.where(low, dot01, dot11), axis=1, keepdims=True)
    stat_b = jnp.sum(jnp.where(low, form, dot00), axis=1, keepdims=True)
    stats = jnp.where((lane < 16) & ((row128 >> 2) == core), g2, 0.0)
    stats = jnp.where(lane == 16 + 2 * core, stat_a, stats)
    stats = jnp.where(lane == 17 + 2 * core, stat_b, stats)
    az2[core, region] = stats
    z2 = [send(az2.at[core, region], az2.at[core, region], z2_send.at[7, 0], z2_recv.at[7, 0], sibling)]
    for d in range(1, 8):
        for cc in (0, 1):
            z2.append(
                send(
                    az2.at[core, region], az2.at[core, region], z2_send.at[d - 1, cc], z2_recv.at[d - 1, core],
                    z_peer(d, cc),
                )
            )
    sib_pack = send(packed.at[pl.ds(2 * other, 2)], sib_packed, sib_send.at[2], sib_recv.at[2], sibling)

    results = []
    for i in range(4):
        yb = apply(split(targets[2 * i]), 4 + i, NN)
        results.append(jnp.where(low, dense[i, 0], yb))
    results = jnp.concatenate(results, axis=0)
    high = results.astype(BF16)
    less = (results - high.astype(F32)).astype(BF16)
    s = lax.dot_general(w3, high, NN, preferred_element_type=F32)
    s = s + lax.dot_general(w3, less, NN, preferred_element_type=F32)
    dense[...] = s.reshape(16, 2, 8, BLK)
    landed[here] = dense[chip, core]
    send(dense.at[chip, other], landed.at[here], rs_send.at[15, 0], rs_recv.at[15, 0], sibling)
    for n, (dy, dx) in enumerate(PLANE):
        for cc in (0, 1):
            send(
                dense.at[plane_chip(dy, dx), cc], landed.at[here], rs_send.at[n, cc], rs_recv.at[n, core],
                plane_peer(dy, dx, cc),
            )

    def waiting(dst, ssem, rsem):
        return pltpu.make_async_remote_copy(
            src_ref=dst, dst_ref=dst, send_sem=ssem, recv_sem=rsem, device_id=sibling, device_id_type=MESH
        )

    z2[0].wait_recv()
    for d in range(1, 8):
        for cc in (0, 1):
            waiting(
                az2.at[cc, lax.rem(region + 8 - d, 8)], z2_send.at[d - 1, cc], z2_recv.at[d - 1, cc]
            ).wait_recv()
    t = az2[0, 0]
    for i in range(1, 16):
        t = t + az2[i // 8, i % 8]
    ap2[chip] = t
    a2 = []
    for n, (dy, dx) in enumerate(PLANE):
        a2.append(send(ap2.at[chip], ap2.at[chip], p2_send.at[n], p2_recv.at[n], plane_peer(dy, dx, core)))

    sib_pack.wait_recv()
    waiting(landed.at[other * 16 + chip], rs_send.at[15, 0], rs_recv.at[15, 0]).wait_recv()
    for n, (dy, dx) in enumerate(PLANE):
        for cc in (0, 1):
            waiting(
                landed.at[cc * 16 + plane_chip(-dy % 4, -dx % 4)], rs_send.at[n, cc], rs_recv.at[n, cc]
            ).wait_recv()
    total = []
    for cc in (0, 1):
        s = landed[cc * 16]
        for i in range(1, 16):
            s = s + landed[cc * 16 + i]
        total.append(s)
    w1s, w2s = [], []
    for b in (0, 1):
        mine, theirs = packed[2 * core + b], sib_packed[b]
        c0 = jnp.where(core == 0, mine, theirs)
        c1 = jnp.where(core == 0, theirs, mine)
        w1s.append(jnp.where(low, c0, flip(c1)))
        z = jnp.where(low, flip(c0), c1)
        pair = jnp.where(low, total[0], flip(total[1])) if b == 0 else jnp.where(low, flip(total[0]), total[1])
        w2s.append(z + pair)

    arrive(a2)
    t = ap2[0]
    for i in range(1, 16):
        t = t + ap2[i]
    a0, b0 = jnp.broadcast_to(t[:, 16:17], (8, 128)), jnp.broadcast_to(t[:, 17:18], (8, 128))
    a1, b1 = jnp.broadcast_to(t[:, 18:19], (8, 128)), jnp.broadcast_to(t[:, 19:20], (8, 128))
    squares = jnp.sum(jnp.where(lane < 16, t * t, 0.0), axis=1, keepdims=True)
    m1 = jnp.where(low128, a0, flip(a1))
    m2 = jnp.where(low128, flip(a0), a1)
    m3 = jnp.where(low128, b0, flip(b1)) + squares
    m0 = jnp.where(low128, flip(b0), b1)
    alpha = m0 / m1
    fresh = m0 - 2.0 * alpha * m1 + alpha * alpha * m2
    grow = 1.0 + fresh / m0
    curve = grow * grow * m1 - 2.0 * grow * alpha * m2 + alpha * alpha * m3
    alpha2 = fresh / curve
    ca = (alpha + alpha2 * grow)[:, 0:1]
    cb = (alpha * alpha2)[:, 0:1]
    for b in (0, 1):
        r0, w1 = probes[b], w1s[b]
        f = features[b]
        w2 = w2s[b]
        for i in range(16):
            w2 = w2 + t[:, i : i + 1] * f[i : i + 1, :]
        out_sol[b] = ca * r0 - cb * w1
        out_res[b] = r0 - ca * w1 + cb * w2
    for c in sends:
        c.wait_send()


def shards(probes, coords, features, noise_var, inv_scale, owner_map, block_pairs):
    vmem = pl.BlockSpec(memory_space=pltpu.VMEM)
    smem = pl.BlockSpec(memory_space=pltpu.SMEM)
    dma = pltpu.SemaphoreType.DMA
    out = jax.ShapeDtypeStruct(probes.shape, F32)
    coords = jnp.transpose(coords, (1, 0, 2))
    block_pairs = jnp.transpose(block_pairs, (0, 2, 1))
    pairs_of = []
    for shape in ((15,), (16,), (15,), (3,), (2, 2, 3), (16, 2), (7,), (15,), (8, 2), (15,)):
        pairs_of += [dma(shape), dma(shape)]
    return pl.pallas_call(
        kernel,
        out_shape=(out, out),
        in_specs=[vmem, vmem, vmem, vmem, smem, smem, smem, vmem, vmem],
        out_specs=(vmem, vmem),
        scratch_shapes=[
            pltpu.VMEM((32, 8, BLK), F32),
            pltpu.VMEM((16, 2, 8, BLK), F32),
            pltpu.VMEM((2, 8, BLK), F32),
            pltpu.VMEM((2, 16, BLK), F32),
            pltpu.VMEM((96, 8, BLK), F32),
            pltpu.VMEM((16, 2, 8, BLK), F32),
            pltpu.VMEM((32, 8, BLK), F32),
            pltpu.VMEM((8, BLK, BLK), BF16),
            pltpu.VMEM((8, BLK, BLK), BF16),
            pltpu.VMEM((BLK, 8), F32),
            pltpu.VMEM((4, 16, BLK), BF16),
            pltpu.VMEM((4, 16, BLK), BF16),
            pltpu.VMEM((96, 768), F32),
            pltpu.VMEM((96, 768), BF16),
            pltpu.VMEM((4, 8, BLK), F32),
            pltpu.VMEM((12, 8, BLK), F32),
            pltpu.VMEM((4, 8, BLK), F32),
            pltpu.VMEM((2, 8, BLK), F32),
            pltpu.VMEM((8, 128), F32),
            pltpu.VMEM((8, 8, 128), F32),
            pltpu.VMEM((16, 8, 128), F32),
            pltpu.VMEM((2, 8, 8, 128), F32),
            pltpu.VMEM((16, 8, 128), F32),
        ]
        + pairs_of,
        compiler_params=pltpu.CompilerParams(
            collective_id=0, has_side_effects=True, vmem_limit_bytes=40 << 20
        ),
        name="cg2",
    )(probes, coords, features, noise_var, inv_scale, owner_map, block_pairs, owner_map, block_pairs)


def solution(mesh):
    return jax.shard_map(
        shards,
        mesh=mesh,
        in_specs=(
            P(("region", "dev"), None, None),
            P(("region", "dev"), None, None),
            P(("region", "dev"), None, None),
            P(("region", "dev"), None),
            P(),
            P("region", None),
            P("region", None, None),
        ),
        out_specs=(P(("region", "dev"), None, None), P(("region", "dev"), None, None)),
        check_vma=False,
    )
```

```python
import jax
import jax.numpy as jnp
from jax import lax
from jax.experimental import pallas as pl
from jax.experimental.pallas import tpu as pltpu
from jax.sharding import PartitionSpec as P

MESH = pl.DeviceIdType.MESH
F32 = jnp.float32
BF16 = jnp.bfloat16
BLK = 512
NT = (((1,), (1,)), ((), ()))
NN = (((1,), (0,)), ((), ()))
PLANE = [(dy, dx) for dy in range(4) for dx in range(4) if dy or dx]


def kernel(
    probes_in, coords_in, features_in, noise_in, inv_scale_in, owner_in, pairs_in,
    out,
    probes, coords, features, noise, inv_scale, owner_s, pairs_s, owner_v, pairs_v, in_sem,
    points, field, halves, cross, sib_cross, v2, dense, landed, kh, kl, turned, fh, fl, w2f, w2b, diag, targets,
    tile, az1, ac1, ap1, az2, ap2,
    pt_send, pt_recv, pf_send, pf_recv, fd_send, fd_recv, sib_send, sib_recv, ag_send, ag_recv,
    rs_send, rs_recv, z1_send, z1_recv, p1_send, p1_recv, z2_send, z2_recv, p2_send, p2_recv,
):
    region = lax.axis_index("region")
    dev = lax.axis_index("dev")
    y, x, core = dev // 8, (dev // 2) % 4, dev % 2
    other = 1 - core
    chip = y * 4 + x
    pos = (chip, x * 4 + y)

    def plane_chip(dy, dx):
        return lax.rem(y + dy, 4) * 4 + lax.rem(x + dx, 4)

    def plane_peer(dy, dx, cc):
        return (region, plane_chip(dy, dx) * 2 + cc)

    def z_peer(d, cc):
        return (lax.rem(region + d, 8), chip * 2 + cc)

    sibling = (region, chip * 2 + other)

    loads_in = []
    for src, dst in (
        (coords_in, coords), (noise_in, noise), (probes_in, probes), (features_in, features), (inv_scale_in, inv_scale),
        (owner_in, owner_v), (pairs_in, pairs_v), (owner_in, owner_s), (pairs_in, pairs_s),
    ):
        c = pltpu.make_async_copy(src, dst, in_sem.at[len(loads_in)])
        c.start()
        loads_in.append(c)

    barrier = pltpu.get_barrier_semaphore()
    for dy, dx in PLANE:
        pl.semaphore_signal(barrier, inc=1, device_id=plane_peer(dy, dx, core), device_id_type=MESH)
    for d in range(1, 8):
        pl.semaphore_signal(barrier, inc=1, device_id=z_peer(d, core), device_id_type=MESH)
    pl.semaphore_signal(barrier, inc=1, device_id=sibling, device_id_type=MESH)

    row = lax.broadcasted_iota(jnp.int32, (8, BLK), 0)
    low = row < 4
    lane = lax.broadcasted_iota(jnp.int32, (8, 128), 1)
    row128 = lax.broadcasted_iota(jnp.int32, (8, 128), 0)
    low128 = row128 < 4

    def flip(v):
        return pltpu.roll(v, 4, 0)

    for c in loads_in:
        c.wait()
    here = core * 16 + chip
    for b in (0, 1):
        for d in range(3):
            points[here, 4 * b + d : 4 * b + d + 1, :] = coords[d, b : b + 1, :]
        points[here, 4 * b + 3 : 4 * b + 4, :] = noise[b : b + 1, :]
    p0, p1 = probes[0], probes[1]
    halves[0] = jnp.where(low, p0, flip(p1))
    halves[1] = jnp.where(low, flip(p0), p1)
    field[chip, core] = halves[core]

    pl.semaphore_wait(barrier, 23)

    sends = []

    def send(src, dst, ssem, rsem, device):
        c = pltpu.make_async_remote_copy(
            src_ref=src, dst_ref=dst, send_sem=ssem, recv_sem=rsem, device_id=device, device_id_type=MESH
        )
        c.start()
        sends.append(c)
        return c

    def arrive(copies):
        for c in copies:
            c.wait_recv()

    sib_field = send(halves.at[other], field.at[chip, core], sib_send.at[0], sib_recv.at[0], sibling)
    point_copies = []
    for n, (dy, dx) in enumerate(PLANE):
        point_copies.append(
            send(points.at[here], points.at[here], pt_send.at[n], pt_recv.at[n], plane_peer(dy, dx, core))
        )
    forwards = [send(points.at[here], points.at[here], pf_send.at[15], pf_recv.at[15], sibling)]

    sx, sy, st = inv_scale[0], inv_scale[1], inv_scale[2]

    def make_tile(index, left, right):
        turned[...] = jnp.transpose(left)
        rx, ry, rt = right[0:1, :] * sx, right[1:2, :] * sy, right[2:3, :] * st

        def rows(i, _):
            span = pl.ds(pl.multiple_of(i * 16, 16), 16)
            part = turned[span, :]
            dx = part[:, 0:1] * sx - rx
            dy = part[:, 1:2] * sy - ry
            dt = part[:, 2:3] * st - rt
            sq = jnp.maximum(dx * dx + dy * dy, 1e-30)
            a = jnp.maximum(1.0 - sq * lax.rsqrt(sq), 0.0)
            b = jnp.maximum(1.0 - jnp.abs(dt), 0.0)
            m = a * b
            m = m * m
            m = m * m
            value = m * ((1.25 - a) * (1.25 - b))
            high = value.astype(BF16)
            kh[index, span, :] = high
            kl[index, span, :] = (value - high.astype(F32)).astype(BF16)
            return 0

        lax.fori_loop(0, 32, rows, 0, unroll=32)

    def points_of(index, b):
        v = points[index]
        if isinstance(b, int):
            return v if b == 0 else flip(v)
        return jnp.where(b == 0, v, flip(v))

    def field_of(q, c, b):
        v = field[q, c]
        f = flip(v)
        first, second = jnp.where(low, v, f), jnp.where(low, f, v)
        if isinstance(b, int):
            return first if b == 0 else second
        return jnp.where(b == 0, first, second)

    def split(v):
        high = v.astype(BF16).astype(F32)
        return jnp.where(low, high, v - high).astype(BF16)

    def fold(v, high, rest, dims):
        s = lax.dot_general(v, high, dims, preferred_element_type=F32)
        s = s + lax.dot_general(v, rest, dims, preferred_element_type=F32)
        return s + flip(s)

    def apply(v, index, dims):
        return 4.0 * fold(v, kh[index], kl[index], dims)

    for b in (0, 1):
        f = features[b]
        high = f.astype(BF16)
        fh[b] = high
        fl[b] = (f - high.astype(F32)).astype(BF16)

    def stack(v):
        top = v.astype(BF16).astype(F32)
        return jnp.concatenate([top, v - top], axis=0).astype(BF16)

    def unstack(v, high, rest, dims):
        d = lax.dot_general(v, high, dims, preferred_element_type=F32)
        d = d + lax.dot_general(v, rest, dims, preferred_element_type=F32)
        return d[0:8] + d[8:16]

    def loads(v0, v1):
        tile[:, 0:16] = unstack(v0, fh[0], fl[0], NT) + unstack(v1, fh[1], fl[1], NT)
        return tile[...]

    tile[...] = jnp.zeros_like(tile)
    first_stack = [stack(probes[b]) for b in (0, 1)]
    az1[region] = loads(*first_stack)
    z1 = []
    for d in range(1, 8):
        z1.append(send(az1.at[region], az1.at[region], z1_send.at[d - 1], z1_recv.at[d - 1], z_peer(d, core)))

    sib_field.wait_recv()
    field_copies = []
    for n, (dy, dx) in enumerate(PLANE):
        field_copies.append(
            send(field.at[chip], field.at[chip], fd_send.at[n], fd_recv.at[n], plane_peer(dy, dx, core))
        )

    mine0 = points[here]
    make_tile(0, mine0, mine0)
    mine1 = flip(mine0)
    make_tile(1, mine1, mine1)

    lane64 = lax.broadcasted_iota(jnp.int32, (64, 64), 1)
    owner_row = owner_v[...].astype(F32)
    ids = jnp.transpose(pairs_v[0].astype(F32)).astype(jnp.int32)
    slot_a = jnp.sum(jnp.where(ids[:, 0:1] == lane64, owner_row, 0.0), axis=1, keepdims=True)
    slot_b = jnp.sum(jnp.where(ids[:, 1:2] == lane64, owner_row, 0.0), axis=1, keepdims=True)
    first, second = [], []
    for i in range(4):
        first.append(owner_s[0, pairs_s[0, 0, chip * 4 + i]])
        second.append(owner_s[0, pairs_s[0, 1, chip * 4 + i]])

    j = lax.broadcasted_iota(jnp.int32, (1, 768), 1)
    n = j >> 3
    side = (j >> 2) & 1
    h = (n >= 48).astype(jnp.int32)
    rest = n - h * 48
    place = (rest * 171) >> 9
    e = rest - place * 3
    q = jnp.where(h == 0, place, (place & 3) * 4 + (place >> 2))
    pick = lax.broadcasted_iota(jnp.int32, (64, 768), 0) == q * 4 + h * 2 + e
    listed = jnp.sum(jnp.where(pick, jnp.where(side == 0, slot_a, slot_b), 0.0), axis=0, keepdims=True)
    lanes2 = jnp.where(e == 2, (q * 4 + side * 2 + h).astype(F32), listed)
    same_column = (lax.broadcasted_iota(jnp.int32, (8, 768), 0) & 3) == (j & 3)
    wanted = []
    for i in range(4):
        wanted += [first[i], second[i]]
    for k in range(8):
        hit = (lanes2 == wanted[k].astype(F32)) & same_column
        w2f[8 * k : 8 * k + 8, :] = jnp.where(hit, 1.0, 0.0)
    block_of_row = lax.broadcasted_iota(jnp.int32, (8, 768), 0) >> 2
    for k in (0, 1):
        hit = (lanes2 == (chip * 4 + 2 * k + block_of_row).astype(F32)) & same_column
        w2f[64 + 8 * k : 72 + 8 * k, :] = jnp.where(hit, 1.0, 0.0)
    w2b[...] = w2f[...].astype(BF16)
    factor = []
    for b in (0, 1):
        me = (dev * 2 + b).astype(F32)
        count = jnp.where(slot_a == me, 1.0, 0.0) + jnp.where(slot_b == me, 1.0, 0.0)
        factor.append(1.0 + jnp.sum(count, axis=0, keepdims=True))
    lane32 = lax.broadcasted_iota(jnp.int32, (256, 32), 1)
    slot32 = jnp.zeros((256, 32), jnp.int32)
    for i in range(8):
        slot32 = jnp.where((lane32 >> 2) == i, wanted[i], slot32)
    row32 = lax.broadcasted_iota(jnp.int32, (256, 32), 0)
    w3 = jnp.where((slot32 == (row32 >> 2)) & ((lane32 & 3) == (row32 & 3)), 1.0, 0.0).astype(BF16)

    arrive(z1)
    t = az1[0]
    for i in range(1, 8):
        t = t + az1[i]
    ac1[0] = t
    sib_loads = send(ac1.at[0], ac1.at[1], sib_send.at[3], sib_recv.at[3], sibling)
    for n, (dy, dx) in enumerate(PLANE):
        back = core * 16 + plane_chip(-dy % 4, -dx % 4)
        point_copies[n].wait_recv()
        forwards.append(send(points.at[back], points.at[back], pf_send.at[n], pf_recv.at[n], sibling))

    sib_loads.wait_recv()
    ap1[chip] = ac1[0] + ac1[1]
    a1 = []
    for n, (dy, dx) in enumerate(PLANE):
        a1.append(send(ap1.at[chip], ap1.at[chip], p1_send.at[n], p1_recv.at[n], plane_peer(dy, dx, core)))

    for b in (0, 1):
        diag[b] = factor[b] * (4.0 * unstack(first_stack[b], kh[b], kl[b], NN)) + noise[b : b + 1, :] * probes[b]

    arrive(forwards)

    def where_is(s):
        return s >> 2, (s >> 1) & 1, s & 1

    for i in range(4):
        qa, ca, ba = where_is(first[i])
        qb, cb, bb = where_is(second[i])
        make_tile(2 + i, points_of(ca * 16 + qa, ba), points_of(cb * 16 + qb, bb))

    arrive(a1)
    g1 = ap1[0]
    for i in range(1, 16):
        g1 = g1 + ap1[i]

    def spread(g, f, acc):
        for i in range(16):
            acc = acc + g[:, i : i + 1] * f[i : i + 1, :]
        return acc

    d0 = spread(g1, features[0], diag[0])
    d1 = spread(g1, features[1], diag[1])
    cross[0] = jnp.where(low, d0, flip(d1))
    cross[1] = jnp.where(low, flip(d0), d1)
    sib_diag = send(cross.at[other], sib_cross.at[0], sib_send.at[1], sib_recv.at[1], sibling)

    arrive(field_copies)
    for i in range(4):
        va, vb = field_of(*where_is(first[i])), field_of(*where_is(second[i]))
        ya = apply(split(vb), 2 + i, NT)
        yb = apply(split(va), 2 + i, NN)
        v2[(i // 2) * 48 + pos[i // 2] * 3 + i % 2] = jnp.where(low, ya, yb)

    def gather_stage(stage_index):
        out = []
        for h in (0, 1):
            if stage_index == 0:
                span = pl.ds(h * 48 + pos[h] * 3, 3)
                steps = [(0, d) if h == 0 else (d, 0) for d in (1, 2, 3)]
            else:
                span = pl.ds(h * 48 + (y, x)[h] * 12, 12)
                steps = [(d, 0) if h == 0 else (0, d) for d in (1, 2, 3)]
            for d, (dy, dx) in enumerate(steps):
                sem = (stage_index, h, d)
                out.append(send(v2.at[span], v2.at[span], ag_send.at[sem], ag_recv.at[sem], plane_peer(dy, dx, core)))
        return out

    sib_diag.wait_recv()
    mine, theirs = cross[core], sib_cross[0]
    c0 = jnp.where(core == 0, mine, theirs)
    c1 = jnp.where(core == 0, theirs, mine)
    v2[pos[0] * 3 + 2] = jnp.where(low, c0, flip(c1))
    v2[48 + pos[1] * 3 + 2] = jnp.where(low, flip(c0), c1)
    arrive(gather_stage(0))
    arrive(gather_stage(1))

    acc = None
    for lo_row in range(0, 768, 256):
        part = v2[lo_row // 8 : lo_row // 8 + 32].reshape(256, BLK)
        w = w2b[:, lo_row : lo_row + 256]
        high = part.astype(BF16)
        less = (part - high.astype(F32)).astype(BF16)
        s = lax.dot_general(w, high, NN, preferred_element_type=F32)
        s = s + lax.dot_general(w, less, NN, preferred_element_type=F32)
        acc = s if acc is None else acc + s
    targets[...] = acc.reshape(10, 8, BLK)
    sib_w1 = send(targets.at[8 + other], sib_cross.at[1], sib_send.at[2], sib_recv.at[2], sibling)

    form = jnp.zeros((8, BLK), F32)
    for i in range(4):
        wa = targets[2 * i]
        ya = apply(split(targets[2 * i + 1]), 2 + i, NT)
        dense[i, 0] = ya
        form = form + 2.0 * (wa * ya)
    form = jnp.where((row >> 2) == core, form, 0.0)
    sib_w1.wait_recv()
    mine, theirs = targets[8 + core], sib_cross[1]
    c0 = jnp.where(core == 0, mine, theirs)
    c1 = jnp.where(core == 0, theirs, mine)
    w1s = [jnp.where(low, c0, flip(c1)), jnp.where(low, flip(c0), c1)]
    stacks = [stack(w) for w in w1s]
    dot00, dot01, dot11 = jnp.zeros((8, BLK), F32), jnp.zeros((8, BLK), F32), jnp.zeros((8, BLK), F32)
    for b in (0, 1):
        r0, w1 = probes[b], w1s[b]
        z = factor[b] * (4.0 * unstack(stacks[b], kh[b], kl[b], NN)) + noise[b : b + 1, :] * w1
        diag[b] = z
        form = form + w1 * z
        dot00 = dot00 + r0 * r0
        dot01 = dot01 + r0 * w1
        dot11 = dot11 + w1 * w1
    stats = loads(*stacks)
    for i, v in enumerate((dot01, dot11, form, dot00)):
        stats = jnp.where(lane == 16 + i, jnp.sum(v, axis=1, keepdims=True), stats)
    az2[core, region] = stats
    z2 = [send(az2.at[core, region], az2.at[core, region], z2_send.at[7, 0], z2_recv.at[7, 0], sibling)]
    for d in range(1, 8):
        for cc in (0, 1):
            z2.append(
                send(
                    az2.at[core, region], az2.at[core, region], z2_send.at[d - 1, cc], z2_recv.at[d - 1, core],
                    z_peer(d, cc),
                )
            )

    results = []
    for i in range(4):
        yb = apply(split(targets[2 * i]), 2 + i, NN)
        results.append(jnp.where(low, dense[i, 0], yb))
    results = jnp.concatenate(results, axis=0)
    high = results.astype(BF16)
    less = (results - high.astype(F32)).astype(BF16)
    s = lax.dot_general(w3, high, NN, preferred_element_type=F32)
    s = s + lax.dot_general(w3, less, NN, preferred_element_type=F32)
    dense[...] = s.reshape(16, 2, 8, BLK)
    landed[here] = dense[chip, core]
    send(dense.at[chip, other], landed.at[here], rs_send.at[15, 0], rs_recv.at[15, 0], sibling)
    for n, (dy, dx) in enumerate(PLANE):
        for cc in (0, 1):
            send(
                dense.at[plane_chip(dy, dx), cc], landed.at[here], rs_send.at[n, cc], rs_recv.at[n, core],
                plane_peer(dy, dx, cc),
            )

    def waiting(dst, ssem, rsem):
        return pltpu.make_async_remote_copy(
            src_ref=dst, dst_ref=dst, send_sem=ssem, recv_sem=rsem, device_id=sibling, device_id_type=MESH
        )

    z2[0].wait_recv()
    for d in range(1, 8):
        for cc in (0, 1):
            waiting(
                az2.at[cc, lax.rem(region + 8 - d, 8)], z2_send.at[d - 1, cc], z2_recv.at[d - 1, cc]
            ).wait_recv()
    t = az2[0, 0]
    for i in range(1, 16):
        t = t + az2[i // 8, i % 8]
    ap2[chip] = t
    a2 = []
    for n, (dy, dx) in enumerate(PLANE):
        a2.append(send(ap2.at[chip], ap2.at[chip], p2_send.at[n], p2_recv.at[n], plane_peer(dy, dx, core)))

    waiting(landed.at[other * 16 + chip], rs_send.at[15, 0], rs_recv.at[15, 0]).wait_recv()
    for n, (dy, dx) in enumerate(PLANE):
        for cc in (0, 1):
            waiting(
                landed.at[cc * 16 + plane_chip(-dy % 4, -dx % 4)], rs_send.at[n, cc], rs_recv.at[n, cc]
            ).wait_recv()
    total = []
    for cc in (0, 1):
        s = landed[cc * 16]
        for i in range(1, 16):
            s = s + landed[cc * 16 + i]
        total.append(s)
    w2s = [
        diag[0] + jnp.where(low, total[0], flip(total[1])),
        diag[1] + jnp.where(low, flip(total[0]), total[1]),
    ]

    arrive(a2)
    t = ap2[0]
    for i in range(1, 16):
        t = t + ap2[i]
    squares = jnp.sum(jnp.where(lane < 16, t * t, 0.0), axis=1, keepdims=True)
    m1, m2, m3, m0 = [jnp.broadcast_to(t[:, 16 + i : 17 + i], (8, 128)) for i in range(4)]
    m3 = m3 + squares
    alpha = m0 / m1
    fresh = m0 - 2.0 * alpha * m1 + alpha * alpha * m2
    grow = 1.0 + fresh / m0
    curve = grow * grow * m1 - 2.0 * grow * alpha * m2 + alpha * alpha * m3
    alpha2 = fresh / curve
    ca = (alpha + alpha2 * grow)[:, 0:1]
    cb = (alpha * alpha2)[:, 0:1]
    for b in (0, 1):
        r0, w1 = probes[b], w1s[b]
        w2 = spread(t, features[b], w2s[b])
        out[0, b] = ca * r0 - cb * w1
        out[1, b] = r0 - ca * w1 + cb * w2
    for c in sends:
        c.wait_send()


def shards(probes, coords, features, noise_var, inv_scale, owner_map, block_pairs):
    vmem = pl.BlockSpec(memory_space=pltpu.VMEM)
    dma = pltpu.SemaphoreType.DMA
    out = jax.ShapeDtypeStruct((2,) + probes.shape, F32)
    coords = jnp.transpose(coords, (1, 0, 2))
    block_pairs = jnp.transpose(block_pairs, (0, 2, 1))
    pairs_of = []
    for shape in ((15,), (16,), (15,), (4,), (2, 2, 3), (16, 2), (7,), (15,), (8, 2), (15,)):
        pairs_of += [dma(shape), dma(shape)]
    both = pl.pallas_call(
        kernel,
        out_shape=out,
        in_specs=[pl.BlockSpec(memory_space=pl.ANY)] * 7,
        out_specs=vmem,
        scratch_shapes=[
            pltpu.VMEM((2, 8, BLK), F32),
            pltpu.VMEM((3, 2, BLK), F32),
            pltpu.VMEM((2, 16, BLK), F32),
            pltpu.VMEM((2, BLK), F32),
            pltpu.SMEM((3,), F32),
            pltpu.SMEM((1, 64), jnp.int32),
            pltpu.SMEM((1, 2, 64), jnp.int32),
            pltpu.VMEM((1, 64), jnp.int32),
            pltpu.VMEM((1, 2, 64), jnp.int32),
            dma((9,)),
            pltpu.VMEM((32, 8, BLK), F32),
            pltpu.VMEM((16, 2, 8, BLK), F32),
            pltpu.VMEM((2, 8, BLK), F32),
            pltpu.VMEM((2, 8, BLK), F32),
            pltpu.VMEM((2, 8, BLK), F32),
            pltpu.VMEM((96, 8, BLK), F32),
            pltpu.VMEM((16, 2, 8, BLK), F32),
            pltpu.VMEM((32, 8, BLK), F32),
            pltpu.VMEM((6, BLK, BLK), BF16),
            pltpu.VMEM((6, BLK, BLK), BF16),
            pltpu.VMEM((BLK, 8), F32),
            pltpu.VMEM((2, 16, BLK), BF16),
            pltpu.VMEM((2, 16, BLK), BF16),
            pltpu.VMEM((80, 768), F32),
            pltpu.VMEM((80, 768), BF16),
            pltpu.VMEM((2, 8, BLK), F32),
            pltpu.VMEM((10, 8, BLK), F32),
            pltpu.VMEM((8, 128), F32),
            pltpu.VMEM((8, 8, 128), F32),
            pltpu.VMEM((2, 8, 128), F32),
            pltpu.VMEM((16, 8, 128), F32),
            pltpu.VMEM((2, 8, 8, 128), F32),
            pltpu.VMEM((16, 8, 128), F32),
        ]
        + pairs_of,
        compiler_params=pltpu.CompilerParams(
            collective_id=0, has_side_effects=True, vmem_limit_bytes=62 << 20
        ),
        name="cg2",
    )(probes, coords, features, noise_var, inv_scale, owner_map, block_pairs)
    return both[0], both[1]


def solution(mesh):
    return jax.shard_map(
        shards,
        mesh=mesh,
        in_specs=(
            P(("region", "dev"), None, None),
            P(("region", "dev"), None, None),
            P(("region", "dev"), None, None),
            P(("region", "dev"), None),
            P(),
            P("region", None),
            P("region", None, None),
        ),
        out_specs=(P(("region", "dev"), None, None), P(("region", "dev"), None, None)),
        check_vma=False,
    )
```

```python
import jax
import jax.numpy as jnp
from jax import lax
from jax.experimental import pallas as pl
from jax.experimental.pallas import tpu as pltpu
from jax.sharding import PartitionSpec as P

MESH = pl.DeviceIdType.MESH
F32 = jnp.float32
BF16 = jnp.bfloat16
BLK = 512
NT = (((1,), (1,)), ((), ()))
NN = (((1,), (0,)), ((), ()))
PLANE = [(dy, dx) for dy in range(4) for dx in range(4) if dy or dx]


def kernel(
    probes_in, coords_in, features_in, noise_in, inv_scale_in, owner_in, pairs_in,
    out,
    probes, coords, features, noise, inv_scale, owner_s, pairs_s, owner_v, pairs_v, in_sem,
    points, field, halves, cross, sib_cross, vp, vd, dense, landed, kh, kl, turned, fh, fl, w2f, w2b, diag, targets,
    tile, az1, ac1, ap1, az2, ap2,
    pt_send, pt_recv, pf_send, pf_recv, sib_send, sib_recv, ag_send, ag_recv,
    rs_send, rs_recv, z1_send, z1_recv, p1_send, p1_recv, z2_send, z2_recv, p2_send, p2_recv,
):
    region = lax.axis_index("region")
    dev = lax.axis_index("dev")
    y, x, core = dev // 8, (dev // 2) % 4, dev % 2
    other = 1 - core
    chip = y * 4 + x
    pos = (chip, x * 4 + y)

    def plane_chip(dy, dx):
        return lax.rem(y + dy, 4) * 4 + lax.rem(x + dx, 4)

    def plane_peer(dy, dx, cc):
        return (region, plane_chip(dy, dx) * 2 + cc)

    def z_peer(d, cc):
        return (lax.rem(region + d, 8), chip * 2 + cc)

    sibling = (region, chip * 2 + other)

    barrier = pltpu.get_barrier_semaphore()
    for dy, dx in PLANE:
        pl.semaphore_signal(barrier, inc=1, device_id=plane_peer(dy, dx, core), device_id_type=MESH)
    for d in range(1, 8):
        pl.semaphore_signal(barrier, inc=1, device_id=z_peer(d, core), device_id_type=MESH)
    pl.semaphore_signal(barrier, inc=1, device_id=sibling, device_id_type=MESH)

    loads_in = []
    for src, dst in (
        (coords_in, coords), (noise_in, noise), (probes_in, probes), (features_in, features), (inv_scale_in, inv_scale),
        (owner_in, owner_v), (pairs_in, pairs_v), (owner_in, owner_s), (pairs_in, pairs_s),
    ):
        c = pltpu.make_async_copy(src, dst, in_sem.at[len(loads_in)])
        c.start()
        loads_in.append(c)

    row = lax.broadcasted_iota(jnp.int32, (8, BLK), 0)
    low = row < 4
    lane = lax.broadcasted_iota(jnp.int32, (8, 128), 1)
    row128 = lax.broadcasted_iota(jnp.int32, (8, 128), 0)
    low128 = row128 < 4

    def flip(v):
        return pltpu.roll(v, 4, 0)

    for c in loads_in[:3]:
        c.wait()
    here = core * 16 + chip
    for b in (0, 1):
        for d in range(3):
            points[here, 4 * b + d : 4 * b + d + 1, :] = coords[d, b : b + 1, :]
        points[here, 4 * b + 3 : 4 * b + 4, :] = noise[b : b + 1, :]
    p0, p1 = probes[0], probes[1]
    halves[0] = jnp.where(low, p0, flip(p1))
    halves[1] = jnp.where(low, flip(p0), p1)
    field[core * 16 + lax.select(core == 0, pos[0], pos[1])] = halves[core]

    pl.semaphore_wait(barrier, 23)

    sends = []

    def send(src, dst, ssem, rsem, device):
        c = pltpu.make_async_remote_copy(
            src_ref=src, dst_ref=dst, send_sem=ssem, recv_sem=rsem, device_id=device, device_id_type=MESH
        )
        c.start()
        sends.append(c)
        return c

    def drain():
        for c in sends:
            c.wait_send()
        sends.clear()

    def arrive(copies):
        for c in copies:
            c.wait_recv()

    own_field = field.at[core * 16 + lax.select(core == 0, pos[0], pos[1])]
    sib_field = send(halves.at[other], own_field, sib_send.at[0], sib_recv.at[0], sibling)
    point_copies = []
    for n, (dy, dx) in enumerate(PLANE):
        point_copies.append(
            send(points.at[here], points.at[here], pt_send.at[n], pt_recv.at[n], plane_peer(dy, dx, core))
        )
    forwards = [send(points.at[here], points.at[here], pf_send.at[15], pf_recv.at[15], sibling)]

    def gather_stage(buf, m, call, stage_index):
        out = []
        for h in (0, 1):
            if stage_index == 0:
                span = pl.ds(h * 16 * m + pos[h] * m, m)
                steps = [(0, d) if h == 0 else (d, 0) for d in (1, 2, 3)]
            else:
                span = pl.ds(h * 16 * m + (y, x)[h] * 4 * m, 4 * m)
                steps = [(d, 0) if h == 0 else (0, d) for d in (1, 2, 3)]
            for d, (dy, dx) in enumerate(steps):
                sem = (call, stage_index, h, d)
                out.append(send(buf.at[span], buf.at[span], ag_send.at[sem], ag_recv.at[sem], plane_peer(dy, dx, core)))
        return out

    sib_field.wait_recv()
    field_first = gather_stage(field, 1, 0, 0)

    for c in loads_in[3:]:
        c.wait()
    sx, sy, st = inv_scale[0], inv_scale[1], inv_scale[2]

    def make_tile(index, left, right):
        turned[...] = jnp.transpose(left)
        rx, ry, rt = right[0:1, :] * sx, right[1:2, :] * sy, right[2:3, :] * st

        def rows(i, _):
            span = pl.ds(pl.multiple_of(i * 16, 16), 16)
            part = turned[span, :]
            dx = part[:, 0:1] * sx - rx
            dy = part[:, 1:2] * sy - ry
            dt = part[:, 2:3] * st - rt
            sq = jnp.maximum(dx * dx + dy * dy, 1e-30)
            a = jnp.maximum(1.0 - sq * lax.rsqrt(sq), 0.0)
            b = jnp.maximum(1.0 - jnp.abs(dt), 0.0)
            m = a * b
            m = m * m
            m = m * m
            value = m * ((1.25 - a) * (1.25 - b))
            high = value.astype(BF16)
            kh[index, span, :] = high
            kl[index, span, :] = (value - high.astype(F32)).astype(BF16)
            return 0

        lax.fori_loop(0, 32, rows, 0, unroll=32)

    def points_of(index, b):
        v = points[index]
        if isinstance(b, int):
            return v if b == 0 else flip(v)
        return jnp.where(b == 0, v, flip(v))

    def field_of(q, c, b):
        v = field[c * 16 + jnp.where(c == 0, q, (q & 3) * 4 + (q >> 2))]
        f = flip(v)
        first, second = jnp.where(low, v, f), jnp.where(low, f, v)
        if isinstance(b, int):
            return first if b == 0 else second
        return jnp.where(b == 0, first, second)

    def split(v):
        high = v.astype(BF16).astype(F32)
        return jnp.where(low, high, v - high).astype(BF16)

    def fold(v, high, rest, dims):
        s = lax.dot_general(v, high, dims, preferred_element_type=F32)
        s = s + lax.dot_general(v, rest, dims, preferred_element_type=F32)
        return s + flip(s)

    def apply(v, index, dims):
        return 4.0 * fold(v, kh[index], kl[index], dims)

    for b in (0, 1):
        f = features[b]
        high = f.astype(BF16)
        fh[b] = high
        fl[b] = (f - high.astype(F32)).astype(BF16)

    def stack(v):
        top = v.astype(BF16).astype(F32)
        return jnp.concatenate([top, v - top], axis=0).astype(BF16)

    def unstack(v, high, rest, dims):
        d = lax.dot_general(v, high, dims, preferred_element_type=F32)
        d = d + lax.dot_general(v, rest, dims, preferred_element_type=F32)
        return d[0:8] + d[8:16]

    def loads(v0, v1):
        tile[:, 0:16] = unstack(v0, fh[0], fl[0], NT) + unstack(v1, fh[1], fl[1], NT)
        return tile[...]

    tile[...] = jnp.zeros_like(tile)
    first_stack = [stack(probes[b]) for b in (0, 1)]
    az1[region] = loads(*first_stack)
    z1 = []
    for d in range(1, 8):
        z1.append(send(az1.at[region], az1.at[region], z1_send.at[d - 1], z1_recv.at[d - 1], z_peer(d, core)))

    mine0 = points[here]
    make_tile(0, mine0, mine0)
    mine1 = flip(mine0)
    make_tile(1, mine1, mine1)

    arrive(field_first)
    field_second = gather_stage(field, 1, 0, 1)

    lane64 = lax.broadcasted_iota(jnp.int32, (64, 64), 1)
    owner_row = owner_v[...].astype(F32)
    ids = jnp.transpose(pairs_v[0].astype(F32)).astype(jnp.int32)
    slot_a = jnp.sum(jnp.where(ids[:, 0:1] == lane64, owner_row, 0.0), axis=1, keepdims=True)
    slot_b = jnp.sum(jnp.where(ids[:, 1:2] == lane64, owner_row, 0.0), axis=1, keepdims=True)
    first, second = [], []
    for i in range(4):
        first.append(owner_s[0, pairs_s[0, 0, chip * 4 + i]])
        second.append(owner_s[0, pairs_s[0, 1, chip * 4 + i]])

    j = lax.broadcasted_iota(jnp.int32, (1, 768), 1)
    n = j >> 3
    side = (j >> 2) & 1
    is_pair = n < 64
    h = jnp.where(is_pair, n >> 5, (n >> 4) & 1)
    place = jnp.where(is_pair, (n & 31) >> 1, n & 15)
    e = n & 1
    q = jnp.where(h == 0, place, (place & 3) * 4 + (place >> 2))
    pick = lax.broadcasted_iota(jnp.int32, (64, 768), 0) == q * 4 + h * 2 + e
    listed = jnp.sum(jnp.where(pick, jnp.where(side == 0, slot_a, slot_b), 0.0), axis=0, keepdims=True)
    lanes2 = jnp.where(is_pair, listed, (q * 4 + side * 2 + h).astype(F32))
    same_column = (lax.broadcasted_iota(jnp.int32, (8, 768), 0) & 3) == (j & 3)
    wanted = []
    for i in range(4):
        wanted += [first[i], second[i]]
    for k in range(8):
        hit = (lanes2 == wanted[k].astype(F32)) & same_column
        w2f[8 * k : 8 * k + 8, :] = jnp.where(hit, 1.0, 0.0)
    block_of_row = lax.broadcasted_iota(jnp.int32, (8, 768), 0) >> 2
    for k in (0, 1):
        hit = (lanes2 == (chip * 4 + 2 * k + block_of_row).astype(F32)) & same_column
        w2f[64 + 8 * k : 72 + 8 * k, :] = jnp.where(hit, 1.0, 0.0)
    w2b[...] = w2f[...].astype(BF16)
    factor = []
    for b in (0, 1):
        me = (dev * 2 + b).astype(F32)
        count = jnp.where(slot_a == me, 1.0, 0.0) + jnp.where(slot_b == me, 1.0, 0.0)
        factor.append(1.0 + jnp.sum(count, axis=0, keepdims=True))
    lane32 = lax.broadcasted_iota(jnp.int32, (256, 32), 1)
    slot32 = jnp.zeros((256, 32), jnp.int32)
    for i in range(8):
        slot32 = jnp.where((lane32 >> 2) == i, wanted[i], slot32)
    row32 = lax.broadcasted_iota(jnp.int32, (256, 32), 0)
    w3 = jnp.where((slot32 == (row32 >> 2)) & ((lane32 & 3) == (row32 & 3)), 1.0, 0.0).astype(BF16)

    arrive(z1)
    t = az1[0]
    for i in range(1, 8):
        t = t + az1[i]
    ac1[0] = t
    sib_loads = send(ac1.at[0], ac1.at[1], sib_send.at[3], sib_recv.at[3], sibling)
    for n, (dy, dx) in enumerate(PLANE):
        back = core * 16 + plane_chip(-dy % 4, -dx % 4)
        point_copies[n].wait_recv()
        forwards.append(send(points.at[back], points.at[back], pf_send.at[n], pf_recv.at[n], sibling))

    sib_loads.wait_recv()
    ap1[chip] = ac1[0] + ac1[1]
    a1 = []
    for n, (dy, dx) in enumerate(PLANE):
        a1.append(send(ap1.at[chip], ap1.at[chip], p1_send.at[n], p1_recv.at[n], plane_peer(dy, dx, core)))

    for b in (0, 1):
        diag[b] = factor[b] * (4.0 * unstack(first_stack[b], kh[b], kl[b], NN)) + noise[b : b + 1, :] * probes[b]

    arrive(forwards)

    def where_is(s):
        return s >> 2, (s >> 1) & 1, s & 1

    for i in range(4):
        qa, ca, ba = where_is(first[i])
        qb, cb, bb = where_is(second[i])
        make_tile(2 + i, points_of(ca * 16 + qa, ba), points_of(cb * 16 + qb, bb))

    arrive(field_second)
    for i in range(4):
        va, vb = field_of(*where_is(first[i])), field_of(*where_is(second[i]))
        ya = apply(split(vb), 2 + i, NT)
        yb = apply(split(va), 2 + i, NN)
        vp[(i // 2) * 32 + pos[i // 2] * 2 + i % 2] = jnp.where(low, ya, yb)

    pair_first = gather_stage(vp, 2, 1, 0)

    arrive(a1)
    g1 = ap1[0]
    for i in range(1, 16):
        g1 = g1 + ap1[i]

    def spread(g, f, acc):
        for i in range(16):
            acc = acc + g[:, i : i + 1] * f[i : i + 1, :]
        return acc

    d0 = spread(g1, features[0], diag[0])
    d1 = spread(g1, features[1], diag[1])
    cross[0] = jnp.where(low, d0, flip(d1))
    cross[1] = jnp.where(low, flip(d0), d1)
    sib_diag = send(cross.at[other], sib_cross.at[0], sib_send.at[1], sib_recv.at[1], sibling)
    sib_diag.wait_recv()
    mine, theirs = cross[core], sib_cross[0]
    c0 = jnp.where(core == 0, mine, theirs)
    c1 = jnp.where(core == 0, theirs, mine)
    vd[pos[0]] = jnp.where(low, c0, flip(c1))
    vd[16 + pos[1]] = jnp.where(low, flip(c0), c1)
    diag_first = gather_stage(vd, 1, 2, 0)
    arrive(pair_first)
    older = list(sends)
    sends.clear()
    pair_second = gather_stage(vp, 2, 1, 1)
    arrive(diag_first)
    diag_second = gather_stage(vd, 1, 2, 1)
    for c in older:
        c.wait_send()
    arrive(pair_second)
    arrive(diag_second)

    acc = None
    for lo_row in range(0, 768, 256):
        part = vp[lo_row // 8 : lo_row // 8 + 32] if lo_row < 512 else vd[...]
        part = part.reshape(256, BLK)
        w = w2b[:, lo_row : lo_row + 256]
        high = part.astype(BF16)
        less = (part - high.astype(F32)).astype(BF16)
        s = lax.dot_general(w, high, NN, preferred_element_type=F32)
        s = s + lax.dot_general(w, less, NN, preferred_element_type=F32)
        acc = s if acc is None else acc + s
    targets[...] = acc.reshape(10, 8, BLK)
    sib_w1 = send(targets.at[8 + other], sib_cross.at[1], sib_send.at[2], sib_recv.at[2], sibling)

    form = jnp.zeros((8, BLK), F32)
    for i in range(4):
        wa = targets[2 * i]
        ya = apply(split(targets[2 * i + 1]), 2 + i, NT)
        dense[i, 0] = ya
        form = form + 2.0 * (wa * ya)
    form = jnp.where((row >> 2) == core, form, 0.0)
    sib_w1.wait_recv()
    mine, theirs = targets[8 + core], sib_cross[1]
    c0 = jnp.where(core == 0, mine, theirs)
    c1 = jnp.where(core == 0, theirs, mine)
    w1s = [jnp.where(low, c0, flip(c1)), jnp.where(low, flip(c0), c1)]
    stacks = [stack(w) for w in w1s]
    dot00, dot01, dot11 = jnp.zeros((8, BLK), F32), jnp.zeros((8, BLK), F32), jnp.zeros((8, BLK), F32)
    for b in (0, 1):
        r0, w1 = probes[b], w1s[b]
        z = factor[b] * (4.0 * unstack(stacks[b], kh[b], kl[b], NN)) + noise[b : b + 1, :] * w1
        diag[b] = z
        form = form + w1 * z
        dot00 = dot00 + r0 * r0
        dot01 = dot01 + r0 * w1
        dot11 = dot11 + w1 * w1
    stats = loads(*stacks)
    for i, v in enumerate((dot01, dot11, form, dot00)):
        stats = jnp.where(lane == 16 + i, jnp.sum(v, axis=1, keepdims=True), stats)
    ap2[chip] = stats
    older2 = list(sends)
    sends.clear()
    a2 = []
    for n, (dy, dx) in enumerate(PLANE):
        a2.append(send(ap2.at[chip], ap2.at[chip], p2_send.at[n], p2_recv.at[n], plane_peer(dy, dx, core)))

    results = []
    for i in range(4):
        yb = apply(split(targets[2 * i]), 2 + i, NN)
        results.append(jnp.where(low, dense[i, 0], yb))
    results = jnp.concatenate(results, axis=0)
    high = results.astype(BF16)
    less = (results - high.astype(F32)).astype(BF16)
    s = lax.dot_general(w3, high, NN, preferred_element_type=F32)
    s = s + lax.dot_general(w3, less, NN, preferred_element_type=F32)
    dense[...] = s.reshape(16, 2, 8, BLK)
    landed[here] = dense[chip, core]
    send(dense.at[chip, other], landed.at[here], rs_send.at[15, 0], rs_recv.at[15, 0], sibling)
    for n, (dy, dx) in enumerate(PLANE):
        for cc in (0, 1):
            send(
                dense.at[plane_chip(dy, dx), cc], landed.at[here], rs_send.at[n, cc], rs_recv.at[n, core],
                plane_peer(dy, dx, cc),
            )

    def waiting(dst, ssem, rsem):
        return pltpu.make_async_remote_copy(
            src_ref=dst, dst_ref=dst, send_sem=ssem, recv_sem=rsem, device_id=sibling, device_id_type=MESH
        )

    for c in older2:
        c.wait_send()
    arrive(a2)
    t = ap2[0]
    for i in range(1, 16):
        t = t + ap2[i]
    az2[core, region] = t
    older3 = list(sends)
    sends.clear()
    z2 = [send(az2.at[core, region], az2.at[core, region], z2_send.at[7, 0], z2_recv.at[7, 0], sibling)]
    for d in range(1, 8):
        for cc in (0, 1):
            z2.append(
                send(
                    az2.at[core, region], az2.at[core, region], z2_send.at[d - 1, cc], z2_recv.at[d - 1, core],
                    z_peer(d, cc),
                )
            )

    waiting(landed.at[other * 16 + chip], rs_send.at[15, 0], rs_recv.at[15, 0]).wait_recv()
    for n, (dy, dx) in enumerate(PLANE):
        for cc in (0, 1):
            waiting(
                landed.at[cc * 16 + plane_chip(-dy % 4, -dx % 4)], rs_send.at[n, cc], rs_recv.at[n, cc]
            ).wait_recv()
    total = []
    for cc in (0, 1):
        s = landed[cc * 16]
        for i in range(1, 16):
            s = s + landed[cc * 16 + i]
        total.append(s)
    w2s = [
        diag[0] + jnp.where(low, total[0], flip(total[1])),
        diag[1] + jnp.where(low, flip(total[0]), total[1]),
    ]

    for c in older3:
        c.wait_send()
    z2[0].wait_recv()
    for d in range(1, 8):
        for cc in (0, 1):
            waiting(
                az2.at[cc, lax.rem(region + 8 - d, 8)], z2_send.at[d - 1, cc], z2_recv.at[d - 1, cc]
            ).wait_recv()
    t = az2[0, 0]
    for i in range(1, 16):
        t = t + az2[i // 8, i % 8]
    squares = jnp.sum(jnp.where(lane < 16, t * t, 0.0), axis=1, keepdims=True)
    m1, m2, m3, m0 = [jnp.broadcast_to(t[:, 16 + i : 17 + i], (8, 128)) for i in range(4)]
    m3 = m3 + squares
    alpha = m0 / m1
    fresh = m0 - 2.0 * alpha * m1 + alpha * alpha * m2
    grow = 1.0 + fresh / m0
    curve = grow * grow * m1 - 2.0 * grow * alpha * m2 + alpha * alpha * m3
    alpha2 = fresh / curve
    ca = (alpha + alpha2 * grow)[:, 0:1]
    cb = (alpha * alpha2)[:, 0:1]
    for b in (0, 1):
        r0, w1 = probes[b], w1s[b]
        w2 = spread(t, features[b], w2s[b])
        out[0, b] = ca * r0 - cb * w1
        out[1, b] = r0 - ca * w1 + cb * w2
    drain()


def shards(probes, coords, features, noise_var, inv_scale, owner_map, block_pairs):
    vmem = pl.BlockSpec(memory_space=pltpu.VMEM)
    dma = pltpu.SemaphoreType.DMA
    out = pltpu.VMEM((2,) + probes.shape, F32)
    coords = jnp.transpose(coords, (1, 0, 2))
    block_pairs = jnp.transpose(block_pairs, (0, 2, 1))
    pairs_of = []
    for shape in ((15,), (16,), (4,), (3, 2, 2, 3), (16, 2), (7,), (15,), (8, 2), (15,)):
        pairs_of += [dma(shape), dma(shape)]
    both = pl.pallas_call(
        kernel,
        out_shape=out,
        in_specs=[pl.BlockSpec(memory_space=pl.ANY)] * 7,
        out_specs=vmem,
        scratch_shapes=[
            pltpu.VMEM((2, 8, BLK), F32),
            pltpu.VMEM((3, 2, BLK), F32),
            pltpu.VMEM((2, 16, BLK), F32),
            pltpu.VMEM((2, BLK), F32),
            pltpu.SMEM((3,), F32),
            pltpu.SMEM((1, 64), jnp.int32),
            pltpu.SMEM((1, 2, 64), jnp.int32),
            pltpu.VMEM((1, 64), jnp.int32),
            pltpu.VMEM((1, 2, 64), jnp.int32),
            dma((9,)),
            pltpu.VMEM((32, 8, BLK), F32),
            pltpu.VMEM((32, 8, BLK), F32),
            pltpu.VMEM((2, 8, BLK), F32),
            pltpu.VMEM((2, 8, BLK), F32),
            pltpu.VMEM((2, 8, BLK), F32),
            pltpu.VMEM((64, 8, BLK), F32),
            pltpu.VMEM((32, 8, BLK), F32),
            pltpu.VMEM((16, 2, 8, BLK), F32),
            pltpu.VMEM((32, 8, BLK), F32),
            pltpu.VMEM((6, BLK, BLK), BF16),
            pltpu.VMEM((6, BLK, BLK), BF16),
            pltpu.VMEM((BLK, 8), F32),
            pltpu.VMEM((2, 16, BLK), BF16),
            pltpu.VMEM((2, 16, BLK), BF16),
            pltpu.VMEM((80, 768), F32),
            pltpu.VMEM((80, 768), BF16),
            pltpu.VMEM((2, 8, BLK), F32),
            pltpu.VMEM((10, 8, BLK), F32),
            pltpu.VMEM((8, 128), F32),
            pltpu.VMEM((8, 8, 128), F32),
            pltpu.VMEM((2, 8, 128), F32),
            pltpu.VMEM((16, 8, 128), F32),
            pltpu.VMEM((2, 8, 8, 128), F32),
            pltpu.VMEM((16, 8, 128), F32),
        ]
        + pairs_of,
        compiler_params=pltpu.CompilerParams(
            collective_id=0, has_side_effects=True, vmem_limit_bytes=62 << 20
        ),
        name="cg2",
    )(probes, coords, features, noise_var, inv_scale, owner_map, block_pairs)
    return both[0], both[1]


def solution(mesh):
    return jax.shard_map(
        shards,
        mesh=mesh,
        in_specs=(
            P(("region", "dev"), None, None),
            P(("region", "dev"), None, None),
            P(("region", "dev"), None, None),
            P(("region", "dev"), None),
            P(),
            P("region", None),
            P("region", None, None),
        ),
        out_specs=(P(("region", "dev"), None, None), P(("region", "dev"), None, None)),
        check_vma=False,
    )
```

```python
import jax
import jax.numpy as jnp
from jax import lax
from jax.experimental import pallas as pl
from jax.experimental.pallas import tpu as pltpu
from jax.sharding import PartitionSpec as P

MESH = pl.DeviceIdType.MESH
F32 = jnp.float32
BF16 = jnp.bfloat16
BLK = 512
NT = (((1,), (1,)), ((), ()))
NN = (((1,), (0,)), ((), ()))
PLANE = [(dy, dx) for dy in range(4) for dx in range(4) if dy or dx]

GROUPS = (
    "sib_field",
    "points",
    "field_first",
    "z1",
    "field_second",
    "sib_loads",
    "forward",
    "a1",
    "pair_first",
    "sib_diag",
    "diag_first",
    "pair_second",
    "diag_second",
    "sib_w1",
    "a2",
    "results",
    "z2",
)


def kernel(
    probes_in, coords_in, features_in, noise_in, inv_scale_in, owner_in, pairs_in,
    out,
    probes, coords, features, noise, inv_scale, owner_s, pairs_s, owner_v, pairs_v, in_sem,
    points, field, halves, cross, sib_cross, vp, vd, dense, landed, kh, kl, turned, fh, fl, w2f, w2b, diag, targets,
    tile, az1, ac1, ap1, az2, ap2,
    group_send, group_recv,
):
    region = lax.axis_index("region")
    dev = lax.axis_index("dev")
    y, x, core = dev // 8, (dev // 2) % 4, dev % 2
    other = 1 - core
    chip = y * 4 + x
    pos = (chip, x * 4 + y)

    def plane_chip(dy, dx):
        return lax.rem(y + dy, 4) * 4 + lax.rem(x + dx, 4)

    def plane_peer(dy, dx, cc):
        return (region, plane_chip(dy, dx) * 2 + cc)

    def z_peer(d, cc):
        return (lax.rem(region + d, 8), chip * 2 + cc)

    sibling = (region, chip * 2 + other)

    barrier = pltpu.get_barrier_semaphore()
    for dy, dx in PLANE:
        pl.semaphore_signal(barrier, inc=1, device_id=plane_peer(dy, dx, core), device_id_type=MESH)
    for d in range(1, 8):
        pl.semaphore_signal(barrier, inc=1, device_id=z_peer(d, core), device_id_type=MESH)
    pl.semaphore_signal(barrier, inc=1, device_id=sibling, device_id_type=MESH)

    loads_in = []
    for src, dst in (
        (coords_in, coords), (noise_in, noise), (probes_in, probes), (features_in, features), (inv_scale_in, inv_scale),
        (owner_in, owner_v), (pairs_in, pairs_v), (owner_in, owner_s), (pairs_in, pairs_s),
    ):
        c = pltpu.make_async_copy(src, dst, in_sem.at[len(loads_in)])
        c.start()
        loads_in.append(c)

    row = lax.broadcasted_iota(jnp.int32, (8, BLK), 0)
    low = row < 4
    lane = lax.broadcasted_iota(jnp.int32, (8, 128), 1)
    row128 = lax.broadcasted_iota(jnp.int32, (8, 128), 0)
    low128 = row128 < 4

    def flip(v):
        return pltpu.roll(v, 4, 0)

    for c in loads_in[:3]:
        c.wait()
    here = core * 16 + chip
    for b in (0, 1):
        for d in range(3):
            points[here, 4 * b + d : 4 * b + d + 1, :] = coords[d, b : b + 1, :]
        points[here, 4 * b + 3 : 4 * b + 4, :] = noise[b : b + 1, :]
    p0, p1 = probes[0], probes[1]
    halves[0] = jnp.where(low, p0, flip(p1))
    halves[1] = jnp.where(low, flip(p0), p1)
    field[core * 16 + lax.select(core == 0, pos[0], pos[1])] = halves[core]

    pl.semaphore_wait(barrier, 23)

    def send(group, src, dst, device):
        pltpu.make_async_remote_copy(
            src_ref=src, dst_ref=dst, send_sem=group_send.at[GROUPS.index(group)], recv_sem=group_recv.at[GROUPS.index(group)],
            device_id=device, device_id_type=MESH,
        ).start()

    def whole(group, span):
        return pltpu.make_async_remote_copy(
            src_ref=span, dst_ref=span, send_sem=group_send.at[GROUPS.index(group)], recv_sem=group_recv.at[GROUPS.index(group)],
            device_id=sibling, device_id_type=MESH,
        )

    spans = {}

    def arrive(group):
        whole(group, spans[group]).wait_recv()

    def sent(*groups):
        for group in groups:
            whole(group, spans[group]).wait_send()

    own_field = field.at[core * 16 + lax.select(core == 0, pos[0], pos[1])]
    send("sib_field", halves.at[other], own_field, sibling)
    spans["sib_field"] = halves.at[0]
    for dy, dx in PLANE:
        send("points", points.at[here], points.at[here], plane_peer(dy, dx, core))
    spans["points"] = points.at[pl.ds(0, 15)]

    def gather_stage(name, buf, m, stage_index):
        for h in (0, 1):
            if stage_index == 0:
                span = pl.ds(h * 16 * m + pos[h] * m, m)
                steps = [(0, d) if h == 0 else (d, 0) for d in (1, 2, 3)]
            else:
                span = pl.ds(h * 16 * m + (y, x)[h] * 4 * m, 4 * m)
                steps = [(d, 0) if h == 0 else (0, d) for d in (1, 2, 3)]
            for dy, dx in steps:
                send(name, buf.at[span], buf.at[span], plane_peer(dy, dx, core))
        spans[name] = buf.at[pl.ds(0, 6 * m * (1 if stage_index == 0 else 4))]

    arrive("sib_field")
    gather_stage("field_first", field, 1, 0)

    for c in loads_in[3:]:
        c.wait()
    sx, sy, st = inv_scale[0], inv_scale[1], inv_scale[2]

    def make_tile(index, left, right):
        turned[...] = jnp.transpose(left)
        rx, ry, rt = right[0:1, :] * sx, right[1:2, :] * sy, right[2:3, :] * st

        def rows(i, _):
            span = pl.ds(pl.multiple_of(i * 16, 16), 16)
            part = turned[span, :]
            dx = part[:, 0:1] * sx - rx
            dy = part[:, 1:2] * sy - ry
            dt = part[:, 2:3] * st - rt
            sq = jnp.maximum(dx * dx + dy * dy, 1e-30)
            a = jnp.maximum(1.0 - sq * lax.rsqrt(sq), 0.0)
            b = jnp.maximum(1.0 - jnp.abs(dt), 0.0)
            m = a * b
            m = m * m
            m = m * m
            value = m * ((1.25 - a) * (1.25 - b))
            high = value.astype(BF16)
            kh[index, span, :] = high
            kl[index, span, :] = (value - high.astype(F32)).astype(BF16)
            return 0

        lax.fori_loop(0, 32, rows, 0, unroll=32)

    def points_of(index, b):
        v = points[index]
        if isinstance(b, int):
            return v if b == 0 else flip(v)
        return jnp.where(b == 0, v, flip(v))

    def field_of(q, c, b):
        v = field[c * 16 + jnp.where(c == 0, q, (q & 3) * 4 + (q >> 2))]
        f = flip(v)
        first, second = jnp.where(low, v, f), jnp.where(low, f, v)
        if isinstance(b, int):
            return first if b == 0 else second
        return jnp.where(b == 0, first, second)

    def split(v):
        high = v.astype(BF16).astype(F32)
        return jnp.where(low, high, v - high).astype(BF16)

    def fold(v, high, rest, dims):
        s = lax.dot_general(v, high, dims, preferred_element_type=F32)
        s = s + lax.dot_general(v, rest, dims, preferred_element_type=F32)
        return s + flip(s)

    def apply(v, index, dims):
        return 4.0 * fold(v, kh[index], kl[index], dims)

    for b in (0, 1):
        f = features[b]
        high = f.astype(BF16)
        fh[b] = high
        fl[b] = (f - high.astype(F32)).astype(BF16)

    def stack(v):
        top = v.astype(BF16).astype(F32)
        return jnp.concatenate([top, v - top], axis=0).astype(BF16)

    def unstack(v, high, rest, dims):
        d = lax.dot_general(v, high, dims, preferred_element_type=F32)
        d = d + lax.dot_general(v, rest, dims, preferred_element_type=F32)
        return d[0:8] + d[8:16]

    def loads(v0, v1):
        tile[:, 0:16] = unstack(v0, fh[0], fl[0], NT) + unstack(v1, fh[1], fl[1], NT)
        return tile[...]

    tile[...] = jnp.zeros_like(tile)
    first_stack = [stack(probes[b]) for b in (0, 1)]
    az1[region] = loads(*first_stack)
    for d in range(1, 8):
        send("z1", az1.at[region], az1.at[region], z_peer(d, core))
    spans["z1"] = az1.at[pl.ds(0, 7)]

    mine0 = points[here]
    make_tile(0, mine0, mine0)
    mine1 = flip(mine0)
    make_tile(1, mine1, mine1)

    arrive("field_first")
    gather_stage("field_second", field, 1, 1)

    lane64 = lax.broadcasted_iota(jnp.int32, (64, 64), 1)
    owner_row = owner_v[...].astype(F32)
    ids = jnp.transpose(pairs_v[0].astype(F32)).astype(jnp.int32)
    slot_a = jnp.sum(jnp.where(ids[:, 0:1] == lane64, owner_row, 0.0), axis=1, keepdims=True)
    slot_b = jnp.sum(jnp.where(ids[:, 1:2] == lane64, owner_row, 0.0), axis=1, keepdims=True)
    first, second = [], []
    for i in range(4):
        first.append(owner_s[0, pairs_s[0, 0, chip * 4 + i]])
        second.append(owner_s[0, pairs_s[0, 1, chip * 4 + i]])

    wanted = []
    for i in range(4):
        wanted += [first[i], second[i]]
    factor = []
    for b in (0, 1):
        me = (dev * 2 + b).astype(F32)
        count = jnp.where(slot_a == me, 1.0, 0.0) + jnp.where(slot_b == me, 1.0, 0.0)
        factor.append(1.0 + jnp.sum(count, axis=0, keepdims=True))
    arrive("z1")
    t = az1[0]
    for i in range(1, 8):
        t = t + az1[i]
    ac1[0] = t
    send("sib_loads", ac1.at[0], ac1.at[1], sibling)
    spans["sib_loads"] = ac1.at[0]
    arrive("points")
    slab = points.at[pl.ds(core * 16, 16)]
    send("forward", slab, slab, sibling)
    spans["forward"] = slab

    arrive("sib_loads")
    ap1[chip] = ac1[0] + ac1[1]
    for dy, dx in PLANE:
        send("a1", ap1.at[chip], ap1.at[chip], plane_peer(dy, dx, core))
    spans["a1"] = ap1.at[pl.ds(0, 15)]

    for b in (0, 1):
        diag[b] = factor[b] * (4.0 * unstack(first_stack[b], kh[b], kl[b], NN)) + noise[b : b + 1, :] * probes[b]

    arrive("forward")

    def where_is(s):
        return s >> 2, (s >> 1) & 1, s & 1

    for i in range(4):
        qa, ca, ba = where_is(first[i])
        qb, cb, bb = where_is(second[i])
        make_tile(2 + i, points_of(ca * 16 + qa, ba), points_of(cb * 16 + qb, bb))

    arrive("field_second")
    for i in range(4):
        va, vb = field_of(*where_is(first[i])), field_of(*where_is(second[i]))
        ya = apply(split(vb), 2 + i, NT)
        yb = apply(split(va), 2 + i, NN)
        vp[(i // 2) * 32 + pos[i // 2] * 2 + i % 2] = jnp.where(low, ya, yb)

    gather_stage("pair_first", vp, 2, 0)

    arrive("a1")
    g1 = ap1[0]
    for i in range(1, 16):
        g1 = g1 + ap1[i]

    def spread(g, f, acc):
        for i in range(16):
            acc = acc + g[:, i : i + 1] * f[i : i + 1, :]
        return acc

    d0 = spread(g1, features[0], diag[0])
    d1 = spread(g1, features[1], diag[1])
    cross[0] = jnp.where(low, d0, flip(d1))
    cross[1] = jnp.where(low, flip(d0), d1)
    send("sib_diag", cross.at[other], sib_cross.at[0], sibling)
    spans["sib_diag"] = cross.at[0]
    arrive("sib_diag")
    mine, theirs = cross[core], sib_cross[0]
    c0 = jnp.where(core == 0, mine, theirs)
    c1 = jnp.where(core == 0, theirs, mine)
    vd[pos[0]] = jnp.where(low, c0, flip(c1))
    vd[16 + pos[1]] = jnp.where(low, flip(c0), c1)
    gather_stage("diag_first", vd, 1, 0)
    arrive("pair_first")
    gather_stage("pair_second", vp, 2, 1)
    arrive("diag_first")
    gather_stage("diag_second", vd, 1, 1)
    j = lax.broadcasted_iota(jnp.int32, (1, 768), 1)
    n = j >> 3
    side = (j >> 2) & 1
    is_pair = n < 64
    h = jnp.where(is_pair, n >> 5, (n >> 4) & 1)
    place = jnp.where(is_pair, (n & 31) >> 1, n & 15)
    e = n & 1
    q = jnp.where(h == 0, place, (place & 3) * 4 + (place >> 2))
    pick = lax.broadcasted_iota(jnp.int32, (64, 768), 0) == q * 4 + h * 2 + e
    listed = jnp.sum(jnp.where(pick, jnp.where(side == 0, slot_a, slot_b), 0.0), axis=0, keepdims=True)
    lanes2 = jnp.where(is_pair, listed, (q * 4 + side * 2 + h).astype(F32))
    same_column = (lax.broadcasted_iota(jnp.int32, (8, 768), 0) & 3) == (j & 3)
    for k in range(8):
        hit = (lanes2 == wanted[k].astype(F32)) & same_column
        w2f[8 * k : 8 * k + 8, :] = jnp.where(hit, 1.0, 0.0)
    block_of_row = lax.broadcasted_iota(jnp.int32, (8, 768), 0) >> 2
    for k in (0, 1):
        hit = (lanes2 == (chip * 4 + 2 * k + block_of_row).astype(F32)) & same_column
        w2f[64 + 8 * k : 72 + 8 * k, :] = jnp.where(hit, 1.0, 0.0)
    w2b[...] = w2f[...].astype(BF16)
    lane32 = lax.broadcasted_iota(jnp.int32, (256, 32), 1)
    slot32 = jnp.zeros((256, 32), jnp.int32)
    for i in range(8):
        slot32 = jnp.where((lane32 >> 2) == i, wanted[i], slot32)
    row32 = lax.broadcasted_iota(jnp.int32, (256, 32), 0)
    w3 = jnp.where((slot32 == (row32 >> 2)) & ((lane32 & 3) == (row32 & 3)), 1.0, 0.0).astype(BF16)
    sent("sib_field", "points", "field_first", "z1", "field_second", "sib_loads", "forward", "a1")
    sent("pair_first", "sib_diag", "diag_first")
    arrive("pair_second")
    arrive("diag_second")

    acc = None
    for lo_row in range(0, 768, 256):
        part = vp[lo_row // 8 : lo_row // 8 + 32] if lo_row < 512 else vd[...]
        part = part.reshape(256, BLK)
        w = w2b[:, lo_row : lo_row + 256]
        high = part.astype(BF16)
        less = (part - high.astype(F32)).astype(BF16)
        s = lax.dot_general(w, high, NN, preferred_element_type=F32)
        s = s + lax.dot_general(w, less, NN, preferred_element_type=F32)
        acc = s if acc is None else acc + s
    targets[...] = acc.reshape(10, 8, BLK)
    send("sib_w1", targets.at[8 + other], sib_cross.at[1], sibling)
    spans["sib_w1"] = cross.at[0]

    form = jnp.zeros((8, BLK), F32)
    for i in range(4):
        wa = targets[2 * i]
        ya = apply(split(targets[2 * i + 1]), 2 + i, NT)
        dense[i, 0] = ya
        form = form + 2.0 * (wa * ya)
    form = jnp.where((row >> 2) == core, form, 0.0)
    arrive("sib_w1")
    mine, theirs = targets[8 + core], sib_cross[1]
    c0 = jnp.where(core == 0, mine, theirs)
    c1 = jnp.where(core == 0, theirs, mine)
    w1s = [jnp.where(low, c0, flip(c1)), jnp.where(low, flip(c0), c1)]
    stacks = [stack(w) for w in w1s]
    dot00, dot01, dot11 = jnp.zeros((8, BLK), F32), jnp.zeros((8, BLK), F32), jnp.zeros((8, BLK), F32)
    for b in (0, 1):
        r0, w1 = probes[b], w1s[b]
        z = factor[b] * (4.0 * unstack(stacks[b], kh[b], kl[b], NN)) + noise[b : b + 1, :] * w1
        diag[b] = z
        form = form + w1 * z
        dot00 = dot00 + r0 * r0
        dot01 = dot01 + r0 * w1
        dot11 = dot11 + w1 * w1
    stats = loads(*stacks)
    for i, v in enumerate((dot01, dot11, form, dot00)):
        stats = jnp.where(lane == 16 + i, jnp.sum(v, axis=1, keepdims=True), stats)
    ap2[chip] = stats
    for dy, dx in PLANE:
        send("a2", ap2.at[chip], ap2.at[chip], plane_peer(dy, dx, core))
    spans["a2"] = ap2.at[pl.ds(0, 15)]

    results = []
    for i in range(4):
        yb = apply(split(targets[2 * i]), 2 + i, NN)
        results.append(jnp.where(low, dense[i, 0], yb))
    results = jnp.concatenate(results, axis=0)
    high = results.astype(BF16)
    less = (results - high.astype(F32)).astype(BF16)
    s = lax.dot_general(w3, high, NN, preferred_element_type=F32)
    s = s + lax.dot_general(w3, less, NN, preferred_element_type=F32)
    dense[...] = s.reshape(16, 2, 8, BLK)
    landed[here] = dense[chip, core]
    send("results", dense.at[chip, other], landed.at[here], sibling)
    for dy, dx in PLANE:
        for cc in (0, 1):
            send("results", dense.at[plane_chip(dy, dx), cc], landed.at[here], plane_peer(dy, dx, cc))
    spans["results"] = landed.at[pl.ds(0, 31)]

    sent("pair_second", "diag_second", "sib_w1")
    arrive("a2")
    t = ap2[0]
    for i in range(1, 16):
        t = t + ap2[i]
    mine_z = core * 8 + region
    az2[mine_z] = t
    send("z2", az2.at[mine_z], az2.at[mine_z], sibling)
    for d in range(1, 8):
        for cc in (0, 1):
            send("z2", az2.at[mine_z], az2.at[mine_z], z_peer(d, cc))
    spans["z2"] = az2.at[pl.ds(0, 15)]

    arrive("results")
    total = []
    for cc in (0, 1):
        s = landed[cc * 16]
        for i in range(1, 16):
            s = s + landed[cc * 16 + i]
        total.append(s)
    w2s = [
        diag[0] + jnp.where(low, total[0], flip(total[1])),
        diag[1] + jnp.where(low, flip(total[0]), total[1]),
    ]

    sent("a2", "results")
    arrive("z2")
    t = az2[0]
    for i in range(1, 16):
        t = t + az2[i]
    squares = jnp.sum(jnp.where(lane < 16, t * t, 0.0), axis=1, keepdims=True)
    m1, m2, m3, m0 = [jnp.broadcast_to(t[:, 16 + i : 17 + i], (8, 128)) for i in range(4)]
    m3 = m3 + squares
    alpha = m0 / m1
    fresh = m0 - 2.0 * alpha * m1 + alpha * alpha * m2
    grow = 1.0 + fresh / m0
    curve = grow * grow * m1 - 2.0 * grow * alpha * m2 + alpha * alpha * m3
    alpha2 = fresh / curve
    ca = (alpha + alpha2 * grow)[:, 0:1]
    cb = (alpha * alpha2)[:, 0:1]
    for b in (0, 1):
        r0, w1 = probes[b], w1s[b]
        w2 = spread(t, features[b], w2s[b])
        out[0, b] = ca * r0 - cb * w1
        out[1, b] = r0 - ca * w1 + cb * w2
    sent("z2")


def shards(probes, coords, features, noise_var, inv_scale, owner_map, block_pairs):
    vmem = pl.BlockSpec(memory_space=pltpu.VMEM)
    dma = pltpu.SemaphoreType.DMA
    out = pltpu.VMEM((2,) + probes.shape, F32)
    coords = jnp.transpose(coords, (1, 0, 2))
    block_pairs = jnp.transpose(block_pairs, (0, 2, 1))
    both = pl.pallas_call(
        kernel,
        out_shape=out,
        in_specs=[pl.BlockSpec(memory_space=pl.ANY)] * 7,
        out_specs=vmem,
        scratch_shapes=[
            pltpu.VMEM((2, 8, BLK), F32),
            pltpu.VMEM((3, 2, BLK), F32),
            pltpu.VMEM((2, 16, BLK), F32),
            pltpu.VMEM((2, BLK), F32),
            pltpu.SMEM((3,), F32),
            pltpu.SMEM((1, 64), jnp.int32),
            pltpu.SMEM((1, 2, 64), jnp.int32),
            pltpu.VMEM((1, 64), jnp.int32),
            pltpu.VMEM((1, 2, 64), jnp.int32),
            dma((9,)),
            pltpu.VMEM((32, 8, BLK), F32),
            pltpu.VMEM((32, 8, BLK), F32),
            pltpu.VMEM((2, 8, BLK), F32),
            pltpu.VMEM((2, 8, BLK), F32),
            pltpu.VMEM((2, 8, BLK), F32),
            pltpu.VMEM((64, 8, BLK), F32),
            pltpu.VMEM((32, 8, BLK), F32),
            pltpu.VMEM((16, 2, 8, BLK), F32),
            pltpu.VMEM((32, 8, BLK), F32),
            pltpu.VMEM((6, BLK, BLK), BF16),
            pltpu.VMEM((6, BLK, BLK), BF16),
            pltpu.VMEM((BLK, 8), F32),
            pltpu.VMEM((2, 16, BLK), BF16),
            pltpu.VMEM((2, 16, BLK), BF16),
            pltpu.VMEM((80, 768), F32),
            pltpu.VMEM((80, 768), BF16),
            pltpu.VMEM((2, 8, BLK), F32),
            pltpu.VMEM((10, 8, BLK), F32),
            pltpu.VMEM((8, 128), F32),
            pltpu.VMEM((8, 8, 128), F32),
            pltpu.VMEM((2, 8, 128), F32),
            pltpu.VMEM((16, 8, 128), F32),
            pltpu.VMEM((16, 8, 128), F32),
            pltpu.VMEM((16, 8, 128), F32),
        ]
        + [dma((len(GROUPS),))] * 2,
        compiler_params=pltpu.CompilerParams(
            collective_id=0, has_side_effects=True, vmem_limit_bytes=62 << 20
        ),
        name="cg2",
    )(probes, coords, features, noise_var, inv_scale, owner_map, block_pairs)
    return both[0], both[1]


def solution(mesh):
    return jax.shard_map(
        shards,
        mesh=mesh,
        in_specs=(
            P(("region", "dev"), None, None),
            P(("region", "dev"), None, None),
            P(("region", "dev"), None, None),
            P(("region", "dev"), None),
            P(),
            P("region", None),
            P("region", None, None),
        ),
        out_specs=(P(("region", "dev"), None, None), P(("region", "dev"), None, None)),
        check_vma=False,
    )
```

```python
import jax
import jax.numpy as jnp
from jax import lax
from jax.experimental import pallas as pl
from jax.experimental.pallas import tpu as pltpu
from jax.sharding import PartitionSpec as P

MESH = pl.DeviceIdType.MESH
F32 = jnp.float32
BF16 = jnp.bfloat16
BLK = 512
NT = (((1,), (1,)), ((), ()))
NN = (((1,), (0,)), ((), ()))
PLANE = [(dy, dx) for dy in range(4) for dx in range(4) if dy or dx]

GROUPS = (
    "sib_field",
    "points",
    "field_first",
    "z1",
    "field_second",
    "sib_loads",
    "forward",
    "a1",
    "sib_diag",
    "sib_w1",
    "a2",
    "results",
    "z2",
    "pairs",
    "diag",
) + tuple(n + str(h) + str(d) for n in ("pairs", "diag") for h in (0, 1) for d in (0, 1, 2))


def kernel(
    probes_in, coords_in, features_in, noise_in, inv_scale_in, owner_in, pairs_in,
    out,
    probes, coords, features, noise, inv_scale, owner_s, pairs_s, owner_v, pairs_v, in_sem,
    points, field, halves, cross, sib_cross, vp, vd, dense, landed, kh, kl, turned, fh, fl, w2f, w2b, diag, targets,
    tile, az1, ac1, ap1, az2, ap2,
    group_send, group_recv,
):
    region = lax.axis_index("region")
    dev = lax.axis_index("dev")
    y, x, core = dev // 8, (dev // 2) % 4, dev % 2
    other = 1 - core
    chip = y * 4 + x
    pos = (chip, x * 4 + y)

    def plane_chip(dy, dx):
        return lax.rem(y + dy, 4) * 4 + lax.rem(x + dx, 4)

    def plane_peer(dy, dx, cc):
        return (region, plane_chip(dy, dx) * 2 + cc)

    def z_peer(d, cc):
        return (lax.rem(region + d, 8), chip * 2 + cc)

    sibling = (region, chip * 2 + other)

    barrier = pltpu.get_barrier_semaphore()
    for dy, dx in PLANE:
        pl.semaphore_signal(barrier, inc=1, device_id=plane_peer(dy, dx, core), device_id_type=MESH)
    for d in range(1, 8):
        pl.semaphore_signal(barrier, inc=1, device_id=z_peer(d, core), device_id_type=MESH)
    pl.semaphore_signal(barrier, inc=1, device_id=sibling, device_id_type=MESH)

    loads_in = []
    for src, dst in (
        (coords_in, coords), (noise_in, noise), (probes_in, probes), (features_in, features), (inv_scale_in, inv_scale),
        (owner_in, owner_v), (pairs_in, pairs_v), (owner_in, owner_s), (pairs_in, pairs_s),
    ):
        c = pltpu.make_async_copy(src, dst, in_sem.at[len(loads_in)])
        c.start()
        loads_in.append(c)

    row = lax.broadcasted_iota(jnp.int32, (8, BLK), 0)
    low = row < 4
    lane = lax.broadcasted_iota(jnp.int32, (8, 128), 1)
    row128 = lax.broadcasted_iota(jnp.int32, (8, 128), 0)
    low128 = row128 < 4

    def flip(v):
        return pltpu.roll(v, 4, 0)

    for c in loads_in[:3]:
        c.wait()
    here = core * 16 + chip
    for b in (0, 1):
        for d in range(3):
            points[here, 4 * b + d : 4 * b + d + 1, :] = coords[d, b : b + 1, :]
        points[here, 4 * b + 3 : 4 * b + 4, :] = noise[b : b + 1, :]
    p0, p1 = probes[0], probes[1]
    halves[0] = jnp.where(low, p0, flip(p1))
    halves[1] = jnp.where(low, flip(p0), p1)
    field[core * 16 + lax.select(core == 0, pos[0], pos[1])] = halves[core]

    pl.semaphore_wait(barrier, 23)

    def send(group, src, dst, device):
        pltpu.make_async_remote_copy(
            src_ref=src, dst_ref=dst, send_sem=group_send.at[GROUPS.index(group)], recv_sem=group_recv.at[GROUPS.index(group)],
            device_id=device, device_id_type=MESH,
        ).start()

    def whole(group, span):
        return pltpu.make_async_remote_copy(
            src_ref=span, dst_ref=span, send_sem=group_send.at[GROUPS.index(group)], recv_sem=group_recv.at[GROUPS.index(group)],
            device_id=sibling, device_id_type=MESH,
        )

    spans = {}

    def arrive(group):
        whole(group, spans[group]).wait_recv()

    def sent(*groups):
        for group in groups:
            whole(group, spans[group]).wait_send()

    own_field = field.at[core * 16 + lax.select(core == 0, pos[0], pos[1])]
    send("sib_field", halves.at[other], own_field, sibling)
    spans["sib_field"] = halves.at[0]
    for dy, dx in PLANE:
        send("points", points.at[here], points.at[here], plane_peer(dy, dx, core))
    spans["points"] = points.at[pl.ds(0, 15)]

    def gather_stage(name, buf, m, stage_index):
        for h in (0, 1):
            if stage_index == 0:
                span = pl.ds(h * 16 * m + pos[h] * m, m)
                steps = [(0, d) if h == 0 else (d, 0) for d in (1, 2, 3)]
            else:
                span = pl.ds(h * 16 * m + (y, x)[h] * 4 * m, 4 * m)
                steps = [(d, 0) if h == 0 else (0, d) for d in (1, 2, 3)]
            for dy, dx in steps:
                send(name, buf.at[span], buf.at[span], plane_peer(dy, dx, core))
        spans[name] = buf.at[pl.ds(0, 6 * m * (1 if stage_index == 0 else 4))]

    def steps(h, first):
        return [(0, d) if (h == 0) == first else (d, 0) for d in (1, 2, 3)]

    def gather_start(name, buf, m, h):
        own = buf.at[pl.ds(h * 16 * m + pos[h] * m, m)]
        for d, step in enumerate(steps(h, True)):
            send(name + str(h) + str(d), own, own, plane_peer(*step, core))
            spans[name + str(h) + str(d)] = buf.at[pl.ds(0, m)]
        for step in steps(h, False):
            send(name, own, own, plane_peer(*step, core))

    def gather_pass_on(name, buf, m):
        for d in (0, 2, 1):
            for h in (0, 1):
                arrive(name + str(h) + str(d))
                line, place = ((y, x), (x, y))[h]
                at = h * 16 * m + (line * 4 + lax.rem(place + 3 - d, 4)) * m
                span = buf.at[pl.ds(at, m)]
                for step in steps(h, False):
                    send(name, span, span, plane_peer(*step, core))
        spans[name] = buf.at[pl.ds(0, 24 * m)]

    arrive("sib_field")
    gather_stage("field_first", field, 1, 0)

    for c in loads_in[3:]:
        c.wait()
    sx, sy, st = inv_scale[0], inv_scale[1], inv_scale[2]

    def make_tile(index, left, right):
        turned[...] = jnp.transpose(left)
        rx, ry, rt = right[0:1, :] * sx, right[1:2, :] * sy, right[2:3, :] * st

        def rows(i, _):
            span = pl.ds(pl.multiple_of(i * 16, 16), 16)
            part = turned[span, :]
            dx = part[:, 0:1] * sx - rx
            dy = part[:, 1:2] * sy - ry
            dt = part[:, 2:3] * st - rt
            sq = jnp.maximum(dx * dx + dy * dy, 1e-30)
            a = jnp.maximum(1.0 - sq * lax.rsqrt(sq), 0.0)
            b = jnp.maximum(1.0 - jnp.abs(dt), 0.0)
            m = a * b
            m = m * m
            m = m * m
            value = m * ((1.25 - a) * (1.25 - b))
            high = value.astype(BF16)
            kh[index, span, :] = high
            kl[index, span, :] = (value - high.astype(F32)).astype(BF16)
            return 0

        lax.fori_loop(0, 32, rows, 0, unroll=32)

    def points_of(index, b):
        v = points[index]
        if isinstance(b, int):
            return v if b == 0 else flip(v)
        return jnp.where(b == 0, v, flip(v))

    def field_of(q, c, b):
        v = field[c * 16 + jnp.where(c == 0, q, (q & 3) * 4 + (q >> 2))]
        f = flip(v)
        first, second = jnp.where(low, v, f), jnp.where(low, f, v)
        if isinstance(b, int):
            return first if b == 0 else second
        return jnp.where(b == 0, first, second)

    def split(v):
        high = v.astype(BF16).astype(F32)
        return jnp.where(low, high, v - high).astype(BF16)

    def fold(v, high, rest, dims):
        s = lax.dot_general(v, high, dims, preferred_element_type=F32)
        s = s + lax.dot_general(v, rest, dims, preferred_element_type=F32)
        return s + flip(s)

    def apply(v, index, dims):
        return 4.0 * fold(v, kh[index], kl[index], dims)

    for b in (0, 1):
        f = features[b]
        high = f.astype(BF16)
        fh[b] = high
        fl[b] = (f - high.astype(F32)).astype(BF16)

    def stack(v):
        top = v.astype(BF16).astype(F32)
        return jnp.concatenate([top, v - top], axis=0).astype(BF16)

    def unstack(v, high, rest, dims):
        d = lax.dot_general(v, high, dims, preferred_element_type=F32)
        d = d + lax.dot_general(v, rest, dims, preferred_element_type=F32)
        return d[0:8] + d[8:16]

    def loads(v0, v1):
        tile[:, 0:16] = unstack(v0, fh[0], fl[0], NT) + unstack(v1, fh[1], fl[1], NT)
        return tile[...]

    tile[...] = jnp.zeros_like(tile)
    first_stack = [stack(probes[b]) for b in (0, 1)]
    az1[region] = loads(*first_stack)
    for d in range(1, 8):
        send("z1", az1.at[region], az1.at[region], z_peer(d, core))
    spans["z1"] = az1.at[pl.ds(0, 7)]

    mine0 = points[here]
    make_tile(0, mine0, mine0)
    mine1 = flip(mine0)
    make_tile(1, mine1, mine1)

    arrive("field_first")
    gather_stage("field_second", field, 1, 1)

    lane64 = lax.broadcasted_iota(jnp.int32, (64, 64), 1)
    owner_row = owner_v[...].astype(F32)
    ids = jnp.transpose(pairs_v[0].astype(F32)).astype(jnp.int32)
    slot_a = jnp.sum(jnp.where(ids[:, 0:1] == lane64, owner_row, 0.0), axis=1, keepdims=True)
    slot_b = jnp.sum(jnp.where(ids[:, 1:2] == lane64, owner_row, 0.0), axis=1, keepdims=True)
    first, second = [], []
    for i in range(4):
        first.append(owner_s[0, pairs_s[0, 0, chip * 4 + i]])
        second.append(owner_s[0, pairs_s[0, 1, chip * 4 + i]])

    wanted = []
    for i in range(4):
        wanted += [first[i], second[i]]
    factor = []
    for b in (0, 1):
        me = (dev * 2 + b).astype(F32)
        count = jnp.where(slot_a == me, 1.0, 0.0) + jnp.where(slot_b == me, 1.0, 0.0)
        factor.append(1.0 + jnp.sum(count, axis=0, keepdims=True))
    arrive("z1")
    t = az1[0]
    for i in range(1, 8):
        t = t + az1[i]
    ac1[0] = t
    send("sib_loads", ac1.at[0], ac1.at[1], sibling)
    spans["sib_loads"] = ac1.at[0]
    arrive("points")
    slab = points.at[pl.ds(core * 16, 16)]
    send("forward", slab, slab, sibling)
    spans["forward"] = slab

    arrive("sib_loads")
    ap1[chip] = ac1[0] + ac1[1]
    for dy, dx in PLANE:
        send("a1", ap1.at[chip], ap1.at[chip], plane_peer(dy, dx, core))
    spans["a1"] = ap1.at[pl.ds(0, 15)]

    for b in (0, 1):
        diag[b] = factor[b] * (4.0 * unstack(first_stack[b], kh[b], kl[b], NN)) + noise[b : b + 1, :] * probes[b]

    arrive("forward")

    def where_is(s):
        return s >> 2, (s >> 1) & 1, s & 1

    for i in range(4):
        qa, ca, ba = where_is(first[i])
        qb, cb, bb = where_is(second[i])
        make_tile(2 + i, points_of(ca * 16 + qa, ba), points_of(cb * 16 + qb, bb))

    arrive("field_second")
    for i in range(4):
        va, vb = field_of(*where_is(first[i])), field_of(*where_is(second[i]))
        ya = apply(split(vb), 2 + i, NT)
        yb = apply(split(va), 2 + i, NN)
        vp[(i // 2) * 32 + pos[i // 2] * 2 + i % 2] = jnp.where(low, ya, yb)
        if i % 2:
            gather_start("pairs", vp, 2, i // 2)


    arrive("a1")
    g1 = ap1[0]
    for i in range(1, 16):
        g1 = g1 + ap1[i]

    def spread(g, f, acc):
        for i in range(16):
            acc = acc + g[:, i : i + 1] * f[i : i + 1, :]
        return acc

    d0 = spread(g1, features[0], diag[0])
    d1 = spread(g1, features[1], diag[1])
    cross[0] = jnp.where(low, d0, flip(d1))
    cross[1] = jnp.where(low, flip(d0), d1)
    send("sib_diag", cross.at[other], sib_cross.at[0], sibling)
    spans["sib_diag"] = cross.at[0]
    arrive("sib_diag")
    mine, theirs = cross[core], sib_cross[0]
    c0 = jnp.where(core == 0, mine, theirs)
    c1 = jnp.where(core == 0, theirs, mine)
    vd[pos[0]] = jnp.where(low, c0, flip(c1))
    vd[16 + pos[1]] = jnp.where(low, flip(c0), c1)
    for h in (0, 1):
        gather_start("diag", vd, 1, h)
    gather_pass_on("pairs", vp, 2)
    gather_pass_on("diag", vd, 1)
    j = lax.broadcasted_iota(jnp.int32, (1, 768), 1)
    n = j >> 3
    side = (j >> 2) & 1
    is_pair = n < 64
    h = jnp.where(is_pair, n >> 5, (n >> 4) & 1)
    place = jnp.where(is_pair, (n & 31) >> 1, n & 15)
    e = n & 1
    q = jnp.where(h == 0, place, (place & 3) * 4 + (place >> 2))
    pick = lax.broadcasted_iota(jnp.int32, (64, 768), 0) == q * 4 + h * 2 + e
    listed = jnp.sum(jnp.where(pick, jnp.where(side == 0, slot_a, slot_b), 0.0), axis=0, keepdims=True)
    lanes2 = jnp.where(is_pair, listed, (q * 4 + side * 2 + h).astype(F32))
    same_column = (lax.broadcasted_iota(jnp.int32, (8, 768), 0) & 3) == (j & 3)
    for k in range(8):
        hit = (lanes2 == wanted[k].astype(F32)) & same_column
        w2f[8 * k : 8 * k + 8, :] = jnp.where(hit, 1.0, 0.0)
    block_of_row = lax.broadcasted_iota(jnp.int32, (8, 768), 0) >> 2
    for k in (0, 1):
        hit = (lanes2 == (chip * 4 + 2 * k + block_of_row).astype(F32)) & same_column
        w2f[64 + 8 * k : 72 + 8 * k, :] = jnp.where(hit, 1.0, 0.0)
    w2b[...] = w2f[...].astype(BF16)
    lane32 = lax.broadcasted_iota(jnp.int32, (256, 32), 1)
    slot32 = jnp.zeros((256, 32), jnp.int32)
    for i in range(8):
        slot32 = jnp.where((lane32 >> 2) == i, wanted[i], slot32)
    row32 = lax.broadcasted_iota(jnp.int32, (256, 32), 0)
    w3 = jnp.where((slot32 == (row32 >> 2)) & ((lane32 & 3) == (row32 & 3)), 1.0, 0.0).astype(BF16)
    sent("sib_field", "points", "field_first", "z1", "field_second", "sib_loads", "forward", "a1")
    sent("sib_diag")
    for name in ("pairs", "diag"):
        sent(*(name + str(h) + str(d) for h in (0, 1) for d in (0, 1, 2)))
    arrive("pairs")
    arrive("diag")

    acc = None
    for lo_row in range(0, 768, 256):
        part = vp[lo_row // 8 : lo_row // 8 + 32] if lo_row < 512 else vd[...]
        part = part.reshape(256, BLK)
        w = w2b[:, lo_row : lo_row + 256]
        high = part.astype(BF16)
        less = (part - high.astype(F32)).astype(BF16)
        s = lax.dot_general(w, high, NN, preferred_element_type=F32)
        s = s + lax.dot_general(w, less, NN, preferred_element_type=F32)
        acc = s if acc is None else acc + s
    targets[...] = acc.reshape(10, 8, BLK)
    send("sib_w1", targets.at[8 + other], sib_cross.at[1], sibling)
    spans["sib_w1"] = cross.at[0]

    form = jnp.zeros((8, BLK), F32)
    for i in range(4):
        wa = targets[2 * i]
        ya = apply(split(targets[2 * i + 1]), 2 + i, NT)
        dense[i, 0] = ya
        form = form + 2.0 * (wa * ya)
    form = jnp.where((row >> 2) == core, form, 0.0)
    arrive("sib_w1")
    mine, theirs = targets[8 + core], sib_cross[1]
    c0 = jnp.where(core == 0, mine, theirs)
    c1 = jnp.where(core == 0, theirs, mine)
    w1s = [jnp.where(low, c0, flip(c1)), jnp.where(low, flip(c0), c1)]
    stacks = [stack(w) for w in w1s]
    dot00, dot01, dot11 = jnp.zeros((8, BLK), F32), jnp.zeros((8, BLK), F32), jnp.zeros((8, BLK), F32)
    for b in (0, 1):
        r0, w1 = probes[b], w1s[b]
        z = factor[b] * (4.0 * unstack(stacks[b], kh[b], kl[b], NN)) + noise[b : b + 1, :] * w1
        diag[b] = z
        form = form + w1 * z
        dot00 = dot00 + r0 * r0
        dot01 = dot01 + r0 * w1
        dot11 = dot11 + w1 * w1
    stats = loads(*stacks)
    for i, v in enumerate((dot01, dot11, form, dot00)):
        stats = jnp.where(lane == 16 + i, jnp.sum(v, axis=1, keepdims=True), stats)
    ap2[chip] = stats
    for dy, dx in PLANE:
        send("a2", ap2.at[chip], ap2.at[chip], plane_peer(dy, dx, core))
    spans["a2"] = ap2.at[pl.ds(0, 15)]

    results = []
    for i in range(4):
        yb = apply(split(targets[2 * i]), 2 + i, NN)
        results.append(jnp.where(low, dense[i, 0], yb))
    results = jnp.concatenate(results, axis=0)
    high = results.astype(BF16)
    less = (results - high.astype(F32)).astype(BF16)
    s = lax.dot_general(w3, high, NN, preferred_element_type=F32)
    s = s + lax.dot_general(w3, less, NN, preferred_element_type=F32)
    dense[...] = s.reshape(16, 2, 8, BLK)
    landed[here] = dense[chip, core]
    send("results", dense.at[chip, other], landed.at[here], sibling)
    for dy, dx in PLANE:
        for cc in (0, 1):
            send("results", dense.at[plane_chip(dy, dx), cc], landed.at[here], plane_peer(dy, dx, cc))
    spans["results"] = landed.at[pl.ds(0, 31)]

    sent("pairs", "diag", "sib_w1")
    arrive("a2")
    t = ap2[0]
    for i in range(1, 16):
        t = t + ap2[i]
    mine_z = core * 8 + region
    az2[mine_z] = t
    send("z2", az2.at[mine_z], az2.at[mine_z], sibling)
    for d in range(1, 8):
        for cc in (0, 1):
            send("z2", az2.at[mine_z], az2.at[mine_z], z_peer(d, cc))
    spans["z2"] = az2.at[pl.ds(0, 15)]

    arrive("results")
    total = []
    for cc in (0, 1):
        s = landed[cc * 16]
        for i in range(1, 16):
            s = s + landed[cc * 16 + i]
        total.append(s)
    w2s = [
        diag[0] + jnp.where(low, total[0], flip(total[1])),
        diag[1] + jnp.where(low, flip(total[0]), total[1]),
    ]

    sent("a2", "results")
    arrive("z2")
    t = az2[0]
    for i in range(1, 16):
        t = t + az2[i]
    squares = jnp.sum(jnp.where(lane < 16, t * t, 0.0), axis=1, keepdims=True)
    m1, m2, m3, m0 = [jnp.broadcast_to(t[:, 16 + i : 17 + i], (8, 128)) for i in range(4)]
    m3 = m3 + squares
    alpha = m0 / m1
    fresh = m0 - 2.0 * alpha * m1 + alpha * alpha * m2
    grow = 1.0 + fresh / m0
    curve = grow * grow * m1 - 2.0 * grow * alpha * m2 + alpha * alpha * m3
    alpha2 = fresh / curve
    ca = (alpha + alpha2 * grow)[:, 0:1]
    cb = (alpha * alpha2)[:, 0:1]
    for b in (0, 1):
        r0, w1 = probes[b], w1s[b]
        w2 = spread(t, features[b], w2s[b])
        out[0, b] = ca * r0 - cb * w1
        out[1, b] = r0 - ca * w1 + cb * w2
    sent("z2")


def shards(probes, coords, features, noise_var, inv_scale, owner_map, block_pairs):
    vmem = pl.BlockSpec(memory_space=pltpu.VMEM)
    dma = pltpu.SemaphoreType.DMA
    out = pltpu.VMEM((2,) + probes.shape, F32)
    coords = jnp.transpose(coords, (1, 0, 2))
    block_pairs = jnp.transpose(block_pairs, (0, 2, 1))
    both = pl.pallas_call(
        kernel,
        out_shape=out,
        in_specs=[pl.BlockSpec(memory_space=pl.ANY)] * 7,
        out_specs=vmem,
        scratch_shapes=[
            pltpu.VMEM((2, 8, BLK), F32),
            pltpu.VMEM((3, 2, BLK), F32),
            pltpu.VMEM((2, 16, BLK), F32),
            pltpu.VMEM((2, BLK), F32),
            pltpu.SMEM((3,), F32),
            pltpu.SMEM((1, 64), jnp.int32),
            pltpu.SMEM((1, 2, 64), jnp.int32),
            pltpu.VMEM((1, 64), jnp.int32),
            pltpu.VMEM((1, 2, 64), jnp.int32),
            dma((9,)),
            pltpu.VMEM((32, 8, BLK), F32),
            pltpu.VMEM((32, 8, BLK), F32),
            pltpu.VMEM((2, 8, BLK), F32),
            pltpu.VMEM((2, 8, BLK), F32),
            pltpu.VMEM((2, 8, BLK), F32),
            pltpu.VMEM((64, 8, BLK), F32),
            pltpu.VMEM((32, 8, BLK), F32),
            pltpu.VMEM((16, 2, 8, BLK), F32),
            pltpu.VMEM((32, 8, BLK), F32),
            pltpu.VMEM((6, BLK, BLK), BF16),
            pltpu.VMEM((6, BLK, BLK), BF16),
            pltpu.VMEM((BLK, 8), F32),
            pltpu.VMEM((2, 16, BLK), BF16),
            pltpu.VMEM((2, 16, BLK), BF16),
            pltpu.VMEM((80, 768), F32),
            pltpu.VMEM((80, 768), BF16),
            pltpu.VMEM((2, 8, BLK), F32),
            pltpu.VMEM((10, 8, BLK), F32),
            pltpu.VMEM((8, 128), F32),
            pltpu.VMEM((8, 8, 128), F32),
            pltpu.VMEM((2, 8, 128), F32),
            pltpu.VMEM((16, 8, 128), F32),
            pltpu.VMEM((16, 8, 128), F32),
            pltpu.VMEM((16, 8, 128), F32),
        ]
        + [dma((len(GROUPS),))] * 2,
        compiler_params=pltpu.CompilerParams(
            collective_id=0, has_side_effects=True, vmem_limit_bytes=62 << 20
        ),
        name="cg2",
    )(probes, coords, features, noise_var, inv_scale, owner_map, block_pairs)
    return both[0], both[1]


def solution(mesh):
    return jax.shard_map(
        shards,
        mesh=mesh,
        in_specs=(
            P(("region", "dev"), None, None),
            P(("region", "dev"), None, None),
            P(("region", "dev"), None, None),
            P(("region", "dev"), None),
            P(),
            P("region", None),
            P("region", None, None),
        ),
        out_specs=(P(("region", "dev"), None, None), P(("region", "dev"), None, None)),
        check_vma=False,
    )
```

```python
import jax
import jax.numpy as jnp
from jax import lax
from jax.experimental import pallas as pl
from jax.experimental.pallas import tpu as pltpu
from jax.sharding import PartitionSpec as P

MESH = pl.DeviceIdType.MESH
F32 = jnp.float32
BF16 = jnp.bfloat16
BLK = 512
NT = (((1,), (1,)), ((), ()))
NN = (((1,), (0,)), ((), ()))
PLANE = [(dy, dx) for dy in range(4) for dx in range(4) if dy or dx]

GROUPS = (
    "sib_field",
    "points",
    "field_first",
    "z1",
    "field_second",
    "sib_loads",
    "forward",
    "a1",
    "sib_diag",
    "sib_w1",
    "a2",
    "results",
    "z2",
    "pairs",
    "diag",
) + tuple(n + str(h) + str(d) for n in ("pairs", "diag") for h in (0, 1) for d in (0, 1, 2))


def kernel(
    probes_in, coords_in, features_in, noise_in, inv_scale_in, owner_in, pairs_in,
    out,
    probes, coords, features, noise, inv_scale, owner_s, pairs_s, owner_v, pairs_v, in_sem,
    points, field, halves, cross, sib_cross, vp, vd, dense, landed, kh, kl, turned, left_terms, fh, fl, w2f, w2b, diag, targets,
    tile, az1, ac1, ap1, az2, ap2,
    group_send, group_recv,
):
    region = lax.axis_index("region")
    dev = lax.axis_index("dev")
    y, x, core = dev // 8, (dev // 2) % 4, dev % 2
    other = 1 - core
    chip = y * 4 + x
    pos = (chip, x * 4 + y)

    def plane_chip(dy, dx):
        return lax.rem(y + dy, 4) * 4 + lax.rem(x + dx, 4)

    def plane_peer(dy, dx, cc):
        return (region, plane_chip(dy, dx) * 2 + cc)

    def z_peer(d, cc):
        return (lax.rem(region + d, 8), chip * 2 + cc)

    sibling = (region, chip * 2 + other)

    barrier = pltpu.get_barrier_semaphore()
    for dy, dx in PLANE:
        pl.semaphore_signal(barrier, inc=1, device_id=plane_peer(dy, dx, core), device_id_type=MESH)
    for d in range(1, 8):
        pl.semaphore_signal(barrier, inc=1, device_id=z_peer(d, core), device_id_type=MESH)
    pl.semaphore_signal(barrier, inc=1, device_id=sibling, device_id_type=MESH)

    loads_in = []
    for src, dst in (
        (coords_in, coords), (noise_in, noise), (probes_in, probes), (features_in, features), (inv_scale_in, inv_scale),
        (owner_in, owner_v), (pairs_in, pairs_v), (owner_in, owner_s), (pairs_in, pairs_s),
    ):
        c = pltpu.make_async_copy(src, dst, in_sem.at[len(loads_in)])
        c.start()
        loads_in.append(c)

    row = lax.broadcasted_iota(jnp.int32, (8, BLK), 0)
    low = row < 4
    lane = lax.broadcasted_iota(jnp.int32, (8, 128), 1)
    row128 = lax.broadcasted_iota(jnp.int32, (8, 128), 0)
    low128 = row128 < 4

    def flip(v):
        return pltpu.roll(v, 4, 0)

    for c in loads_in[:3]:
        c.wait()
    here = core * 16 + chip
    for b in (0, 1):
        for d in range(3):
            points[here, 4 * b + d : 4 * b + d + 1, :] = coords[d, b : b + 1, :]
        points[here, 4 * b + 3 : 4 * b + 4, :] = noise[b : b + 1, :]
    p0, p1 = probes[0], probes[1]
    halves[0] = jnp.where(low, p0, flip(p1))
    halves[1] = jnp.where(low, flip(p0), p1)
    field[core * 16 + lax.select(core == 0, pos[0], pos[1])] = halves[core]

    for c in loads_in[3:]:
        c.wait()
    for b in (0, 1):
        f = features[b]
        high = f.astype(BF16)
        fh[b] = high
        fl[b] = (f - high.astype(F32)).astype(BF16)

    def stack(v):
        top = v.astype(BF16).astype(F32)
        return jnp.concatenate([top, v - top], axis=0).astype(BF16)

    def unstack(v, high, rest, dims):
        d = lax.dot_general(v, high, dims, preferred_element_type=F32)
        d = d + lax.dot_general(v, rest, dims, preferred_element_type=F32)
        return d[0:8] + d[8:16]

    def loads(v0, v1):
        tile[:, 0:16] = unstack(v0, fh[0], fl[0], NT) + unstack(v1, fh[1], fl[1], NT)
        return tile[...]

    tile[...] = jnp.zeros_like(tile)
    first_stack = [stack(probes[b]) for b in (0, 1)]
    az1[region] = loads(*first_stack)

    pl.semaphore_wait(barrier, 23)

    def send(group, src, dst, device):
        pltpu.make_async_remote_copy(
            src_ref=src, dst_ref=dst, send_sem=group_send.at[GROUPS.index(group)], recv_sem=group_recv.at[GROUPS.index(group)],
            device_id=device, device_id_type=MESH,
        ).start()

    def whole(group, span):
        return pltpu.make_async_remote_copy(
            src_ref=span, dst_ref=span, send_sem=group_send.at[GROUPS.index(group)], recv_sem=group_recv.at[GROUPS.index(group)],
            device_id=sibling, device_id_type=MESH,
        )

    spans = {}

    def arrive(group):
        whole(group, spans[group]).wait_recv()

    def sent(*groups):
        for group in groups:
            whole(group, spans[group]).wait_send()

    own_field = field.at[core * 16 + lax.select(core == 0, pos[0], pos[1])]
    send("sib_field", halves.at[other], own_field, sibling)
    spans["sib_field"] = halves.at[0]
    for d in range(1, 8):
        send("z1", az1.at[region], az1.at[region], z_peer(d, core))
    spans["z1"] = az1.at[pl.ds(0, 7)]
    for dy, dx in PLANE:
        send("points", points.at[here], points.at[here], plane_peer(dy, dx, core))
    spans["points"] = points.at[pl.ds(0, 15)]

    def gather_stage(name, buf, m, stage_index):
        for h in (0, 1):
            if stage_index == 0:
                span = pl.ds(h * 16 * m + pos[h] * m, m)
                steps = [(0, d) if h == 0 else (d, 0) for d in (1, 2, 3)]
            else:
                span = pl.ds(h * 16 * m + (y, x)[h] * 4 * m, 4 * m)
                steps = [(d, 0) if h == 0 else (0, d) for d in (1, 2, 3)]
            for dy, dx in steps:
                send(name, buf.at[span], buf.at[span], plane_peer(dy, dx, core))
        spans[name] = buf.at[pl.ds(0, 6 * m * (1 if stage_index == 0 else 4))]

    def steps(h, first):
        return [(0, d) if (h == 0) == first else (d, 0) for d in (1, 2, 3)]

    def gather_start(name, buf, m, h):
        own = buf.at[pl.ds(h * 16 * m + pos[h] * m, m)]
        for d, step in enumerate(steps(h, True)):
            send(name + str(h) + str(d), own, own, plane_peer(*step, core))
            spans[name + str(h) + str(d)] = buf.at[pl.ds(0, m)]
        for step in steps(h, False):
            send(name, own, own, plane_peer(*step, core))

    def gather_pass_on(name, buf, m):
        for d in (0, 2, 1):
            for h in (0, 1):
                arrive(name + str(h) + str(d))
                line, place = ((y, x), (x, y))[h]
                at = h * 16 * m + (line * 4 + lax.rem(place + 3 - d, 4)) * m
                span = buf.at[pl.ds(at, m)]
                for step in steps(h, False):
                    send(name, span, span, plane_peer(*step, core))
        spans[name] = buf.at[pl.ds(0, 24 * m)]

    arrive("sib_field")
    gather_stage("field_first", field, 1, 0)

    sx, sy, st = inv_scale[0], inv_scale[1], inv_scale[2]

    one = jnp.ones((1, BLK), F32)

    def parts(v):
        top = v.astype(BF16).astype(F32)
        mid = (v - top).astype(BF16).astype(F32)
        return top, mid, v - top - mid

    def make_tile(index, left, right):
        lt_rows, rt_rows = [], []
        for i, scale in ((0, sx), (1, sy)):
            h, m, l = parts((left[i : i + 1, :] - 0.5) * scale)
            rh, rm, rl = parts((right[i : i + 1, :] - 0.5) * scale)
            lt_rows += [-2.0 * h, -2.0 * h, -2.0 * m, -2.0 * h, -2.0 * l, -2.0 * m]
            rt_rows += [rh, rm, rh, rl, rh, rm]
        for v, rows, is_left in ((left, lt_rows, True), (right, rt_rows, False)):
            a, b = (v[0:1, :] - 0.5) * sx, (v[1:2, :] - 0.5) * sy
            n = list(parts(a * a + b * b))
            rows += n + [one] * 3 if is_left else [one] * 3 + n
        t = jnp.transpose(jnp.concatenate(lt_rows + [jnp.zeros((6, BLK), F32), left], axis=0))
        turned[...] = t
        rm_all = jnp.concatenate(rt_rows + [jnp.zeros((14, BLK), F32)], axis=0).astype(BF16)
        left_terms[...] = jnp.where(lax.broadcasted_iota(jnp.int32, (BLK, 32), 1) < 18, t, 0.0).astype(BF16)
        rt = right[2:3, :] * st

        def rows(i, _):
            span = pl.ds(pl.multiple_of(i * 128, 128), 128)
            sq = lax.dot_general(left_terms[span, :], rm_all, NN, preferred_element_type=F32)
            dt = turned[span, 26:27] * st - rt
            sq = jnp.maximum(sq, 1e-30)
            a = jnp.maximum(1.0 - sq * lax.rsqrt(sq), 0.0)
            b = jnp.maximum(1.0 - jnp.abs(dt), 0.0)
            m = a * b
            m = m * m
            m = m * m
            value = m * ((1.25 - a) * (1.25 - b))
            high = value.astype(BF16)
            kh[index, span, :] = high
            kl[index, span, :] = (value - high.astype(F32)).astype(BF16)
            return 0

        lax.fori_loop(0, 4, rows, 0, unroll=4)

    def points_of(index, b):
        v = points[index]
        if isinstance(b, int):
            return v if b == 0 else flip(v)
        return jnp.where(b == 0, v, flip(v))

    def field_of(q, c, b):
        v = field[c * 16 + jnp.where(c == 0, q, (q & 3) * 4 + (q >> 2))]
        f = flip(v)
        first, second = jnp.where(low, v, f), jnp.where(low, f, v)
        if isinstance(b, int):
            return first if b == 0 else second
        return jnp.where(b == 0, first, second)

    def split(v):
        high = v.astype(BF16).astype(F32)
        return jnp.where(low, high, v - high).astype(BF16)

    def fold(v, high, rest, dims):
        s = lax.dot_general(v, high, dims, preferred_element_type=F32)
        s = s + lax.dot_general(v, rest, dims, preferred_element_type=F32)
        return s + flip(s)

    def apply(v, index, dims):
        return 4.0 * fold(v, kh[index], kl[index], dims)

    mine0 = points[here]
    make_tile(0, mine0, mine0)
    mine1 = flip(mine0)
    make_tile(1, mine1, mine1)

    arrive("field_first")
    gather_stage("field_second", field, 1, 1)

    lane64 = lax.broadcasted_iota(jnp.int32, (64, 64), 1)
    owner_row = owner_v[...].astype(F32)
    ids = jnp.transpose(pairs_v[0].astype(F32)).astype(jnp.int32)
    slot_a = jnp.sum(jnp.where(ids[:, 0:1] == lane64, owner_row, 0.0), axis=1, keepdims=True)
    slot_b = jnp.sum(jnp.where(ids[:, 1:2] == lane64, owner_row, 0.0), axis=1, keepdims=True)
    first, second = [], []
    for i in range(4):
        first.append(owner_s[0, pairs_s[0, 0, chip * 4 + i]])
        second.append(owner_s[0, pairs_s[0, 1, chip * 4 + i]])

    wanted = []
    for i in range(4):
        wanted += [first[i], second[i]]
    factor = []
    for b in (0, 1):
        me = (dev * 2 + b).astype(F32)
        count = jnp.where(slot_a == me, 1.0, 0.0) + jnp.where(slot_b == me, 1.0, 0.0)
        factor.append(1.0 + jnp.sum(count, axis=0, keepdims=True))
    arrive("z1")
    t = az1[0]
    for i in range(1, 8):
        t = t + az1[i]
    ac1[0] = t
    send("sib_loads", ac1.at[0], ac1.at[1], sibling)
    spans["sib_loads"] = ac1.at[0]
    arrive("points")
    slab = points.at[pl.ds(core * 16, 16)]
    send("forward", slab, slab, sibling)
    spans["forward"] = slab

    arrive("sib_loads")
    ap1[chip] = ac1[0] + ac1[1]
    for dy, dx in PLANE:
        send("a1", ap1.at[chip], ap1.at[chip], plane_peer(dy, dx, core))
    spans["a1"] = ap1.at[pl.ds(0, 15)]

    for b in (0, 1):
        diag[b] = factor[b] * (4.0 * unstack(first_stack[b], kh[b], kl[b], NN)) + noise[b : b + 1, :] * probes[b]

    arrive("forward")

    def where_is(s):
        return s >> 2, (s >> 1) & 1, s & 1

    for i in range(4):
        qa, ca, ba = where_is(first[i])
        qb, cb, bb = where_is(second[i])
        make_tile(2 + i, points_of(ca * 16 + qa, ba), points_of(cb * 16 + qb, bb))

    arrive("field_second")
    for i in range(4):
        va, vb = field_of(*where_is(first[i])), field_of(*where_is(second[i]))
        ya = apply(split(vb), 2 + i, NT)
        yb = apply(split(va), 2 + i, NN)
        vp[(i // 2) * 32 + pos[i // 2] * 2 + i % 2] = jnp.where(low, ya, yb)
        if i % 2:
            gather_start("pairs", vp, 2, i // 2)


    arrive("a1")
    g1 = ap1[0]
    for i in range(1, 16):
        g1 = g1 + ap1[i]

    def spread(g, f, acc):
        for i in range(16):
            acc = acc + g[:, i : i + 1] * f[i : i + 1, :]
        return acc

    d0 = spread(g1, features[0], diag[0])
    d1 = spread(g1, features[1], diag[1])
    cross[0] = jnp.where(low, d0, flip(d1))
    cross[1] = jnp.where(low, flip(d0), d1)
    send("sib_diag", cross.at[other], sib_cross.at[0], sibling)
    spans["sib_diag"] = cross.at[0]
    arrive("sib_diag")
    mine, theirs = cross[core], sib_cross[0]
    c0 = jnp.where(core == 0, mine, theirs)
    c1 = jnp.where(core == 0, theirs, mine)
    vd[pos[0]] = jnp.where(low, c0, flip(c1))
    vd[16 + pos[1]] = jnp.where(low, flip(c0), c1)
    for h in (0, 1):
        gather_start("diag", vd, 1, h)
    gather_pass_on("pairs", vp, 2)
    gather_pass_on("diag", vd, 1)
    j = lax.broadcasted_iota(jnp.int32, (1, 768), 1)
    n = j >> 3
    side = (j >> 2) & 1
    is_pair = n < 64
    h = jnp.where(is_pair, n >> 5, (n >> 4) & 1)
    place = jnp.where(is_pair, (n & 31) >> 1, n & 15)
    e = n & 1
    q = jnp.where(h == 0, place, (place & 3) * 4 + (place >> 2))
    pick = lax.broadcasted_iota(jnp.int32, (64, 768), 0) == q * 4 + h * 2 + e
    listed = jnp.sum(jnp.where(pick, jnp.where(side == 0, slot_a, slot_b), 0.0), axis=0, keepdims=True)
    lanes2 = jnp.where(is_pair, listed, (q * 4 + side * 2 + h).astype(F32))
    same_column = (lax.broadcasted_iota(jnp.int32, (8, 768), 0) & 3) == (j & 3)
    for k in range(8):
        hit = (lanes2 == wanted[k].astype(F32)) & same_column
        w2f[8 * k : 8 * k + 8, :] = jnp.where(hit, 1.0, 0.0)
    block_of_row = lax.broadcasted_iota(jnp.int32, (8, 768), 0) >> 2
    for k in (0, 1):
        hit = (lanes2 == (chip * 4 + 2 * k + block_of_row).astype(F32)) & same_column
        w2f[64 + 8 * k : 72 + 8 * k, :] = jnp.where(hit, 1.0, 0.0)
    w2b[...] = w2f[...].astype(BF16)
    lane32 = lax.broadcasted_iota(jnp.int32, (256, 32), 1)
    slot32 = jnp.zeros((256, 32), jnp.int32)
    for i in range(8):
        slot32 = jnp.where((lane32 >> 2) == i, wanted[i], slot32)
    row32 = lax.broadcasted_iota(jnp.int32, (256, 32), 0)
    w3 = jnp.where((slot32 == (row32 >> 2)) & ((lane32 & 3) == (row32 & 3)), 1.0, 0.0).astype(BF16)
    sent("sib_field", "points", "field_first", "z1", "field_second", "sib_loads", "forward", "a1")
    sent("sib_diag")
    for name in ("pairs", "diag"):
        sent(*(name + str(h) + str(d) for h in (0, 1) for d in (0, 1, 2)))
    square = jnp.sum(probes[0] * probes[0] + probes[1] * probes[1], axis=1, keepdims=True)
    arrive("pairs")

    acc = None
    for lo_row in range(0, 768, 256):
        if lo_row == 512:
            arrive("diag")
        part = vp[lo_row // 8 : lo_row // 8 + 32] if lo_row < 512 else vd[...]
        part = part.reshape(256, BLK)
        w = w2b[:, lo_row : lo_row + 256]
        high = part.astype(BF16)
        less = (part - high.astype(F32)).astype(BF16)
        s = lax.dot_general(w, high, NN, preferred_element_type=F32)
        s = s + lax.dot_general(w, less, NN, preferred_element_type=F32)
        acc = s if acc is None else acc + s
    targets[...] = acc.reshape(10, 8, BLK)
    send("sib_w1", targets.at[8 + other], sib_cross.at[1], sibling)
    spans["sib_w1"] = cross.at[0]

    form = jnp.zeros((8, BLK), F32)
    for i in range(4):
        wa = targets[2 * i]
        ya = apply(split(targets[2 * i + 1]), 2 + i, NT)
        dense[i, 0] = ya
        form = form + 2.0 * (wa * ya)
    form = jnp.where((row >> 2) == core, form, 0.0)
    arrive("sib_w1")
    mine, theirs = targets[8 + core], sib_cross[1]
    c0 = jnp.where(core == 0, mine, theirs)
    c1 = jnp.where(core == 0, theirs, mine)
    w1s = [jnp.where(low, c0, flip(c1)), jnp.where(low, flip(c0), c1)]
    stacks = [stack(w) for w in w1s]
    dot01, dot11 = jnp.zeros((8, BLK), F32), jnp.zeros((8, BLK), F32)
    for b in (0, 1):
        r0, w1 = probes[b], w1s[b]
        z = factor[b] * (4.0 * unstack(stacks[b], kh[b], kl[b], NN)) + noise[b : b + 1, :] * w1
        diag[b] = z
        form = form + w1 * z
        dot01 = dot01 + r0 * w1
        dot11 = dot11 + w1 * w1
    stats = loads(*stacks)
    for i, v in enumerate((dot01, dot11, form)):
        stats = jnp.where(lane == 16 + i, jnp.sum(v, axis=1, keepdims=True), stats)
    stats = jnp.where(lane == 19, square, stats)
    ap2[chip] = stats
    for dy, dx in PLANE:
        send("a2", ap2.at[chip], ap2.at[chip], plane_peer(dy, dx, core))
    spans["a2"] = ap2.at[pl.ds(0, 15)]

    results = []
    for i in range(4):
        yb = apply(split(targets[2 * i]), 2 + i, NN)
        results.append(jnp.where(low, dense[i, 0], yb))
    results = jnp.concatenate(results, axis=0)
    high = results.astype(BF16)
    less = (results - high.astype(F32)).astype(BF16)
    s = lax.dot_general(w3, high, NN, preferred_element_type=F32)
    s = s + lax.dot_general(w3, less, NN, preferred_element_type=F32)
    dense[...] = s.reshape(16, 2, 8, BLK)
    landed[here] = dense[chip, core]
    send("results", dense.at[chip, other], landed.at[here], sibling)
    for dy, dx in PLANE:
        for cc in (0, 1):
            send("results", dense.at[plane_chip(dy, dx), cc], landed.at[here], plane_peer(dy, dx, cc))
    spans["results"] = landed.at[pl.ds(0, 31)]

    sent("pairs", "diag", "sib_w1")
    arrive("a2")
    t = ap2[0]
    for i in range(1, 16):
        t = t + ap2[i]
    mine_z = core * 8 + region
    az2[mine_z] = t
    send("z2", az2.at[mine_z], az2.at[mine_z], sibling)
    for d in range(1, 8):
        for cc in (0, 1):
            send("z2", az2.at[mine_z], az2.at[mine_z], z_peer(d, cc))
    spans["z2"] = az2.at[pl.ds(0, 15)]

    arrive("results")
    total = []
    for cc in (0, 1):
        s = landed[cc * 16]
        for i in range(1, 16):
            s = s + landed[cc * 16 + i]
        total.append(s)
    w2s = [
        diag[0] + jnp.where(low, total[0], flip(total[1])),
        diag[1] + jnp.where(low, flip(total[0]), total[1]),
    ]

    sent("a2", "results")
    arrive("z2")
    t = az2[0]
    for i in range(1, 16):
        t = t + az2[i]
    squares = jnp.sum(jnp.where(lane < 16, t * t, 0.0), axis=1, keepdims=True)
    m1, m2, m3, m0 = [jnp.broadcast_to(t[:, 16 + i : 17 + i], (8, 128)) for i in range(4)]
    m3 = m3 + squares
    alpha = m0 / m1
    fresh = m0 - 2.0 * alpha * m1 + alpha * alpha * m2
    grow = 1.0 + fresh / m0
    curve = grow * grow * m1 - 2.0 * grow * alpha * m2 + alpha * alpha * m3
    alpha2 = fresh / curve
    ca = (alpha + alpha2 * grow)[:, 0:1]
    cb = (alpha * alpha2)[:, 0:1]
    for b in (0, 1):
        r0, w1 = probes[b], w1s[b]
        w2 = spread(t, features[b], w2s[b])
        out[0, b] = ca * r0 - cb * w1
        out[1, b] = r0 - ca * w1 + cb * w2
    sent("z2")


def shards(probes, coords, features, noise_var, inv_scale, owner_map, block_pairs):
    vmem = pl.BlockSpec(memory_space=pltpu.VMEM)
    dma = pltpu.SemaphoreType.DMA
    out = pltpu.VMEM((2,) + probes.shape, F32)
    coords = jnp.transpose(coords, (1, 0, 2))
    block_pairs = jnp.transpose(block_pairs, (0, 2, 1))
    both = pl.pallas_call(
        kernel,
        out_shape=out,
        in_specs=[pl.BlockSpec(memory_space=pl.ANY)] * 7,
        out_specs=vmem,
        scratch_shapes=[
            pltpu.VMEM((2, 8, BLK), F32),
            pltpu.VMEM((3, 2, BLK), F32),
            pltpu.VMEM((2, 16, BLK), F32),
            pltpu.VMEM((2, BLK), F32),
            pltpu.SMEM((3,), F32),
            pltpu.SMEM((1, 64), jnp.int32),
            pltpu.SMEM((1, 2, 64), jnp.int32),
            pltpu.VMEM((1, 64), jnp.int32),
            pltpu.VMEM((1, 2, 64), jnp.int32),
            dma((9,)),
            pltpu.VMEM((32, 8, BLK), F32),
            pltpu.VMEM((32, 8, BLK), F32),
            pltpu.VMEM((2, 8, BLK), F32),
            pltpu.VMEM((2, 8, BLK), F32),
            pltpu.VMEM((2, 8, BLK), F32),
            pltpu.VMEM((64, 8, BLK), F32),
            pltpu.VMEM((32, 8, BLK), F32),
            pltpu.VMEM((16, 2, 8, BLK), F32),
            pltpu.VMEM((32, 8, BLK), F32),
            pltpu.VMEM((6, BLK, BLK), BF16),
            pltpu.VMEM((6, BLK, BLK), BF16),
            pltpu.VMEM((BLK, 32), F32),
            pltpu.VMEM((BLK, 32), BF16),
            pltpu.VMEM((2, 16, BLK), BF16),
            pltpu.VMEM((2, 16, BLK), BF16),
            pltpu.VMEM((80, 768), F32),
            pltpu.VMEM((80, 768), BF16),
            pltpu.VMEM((2, 8, BLK), F32),
            pltpu.VMEM((10, 8, BLK), F32),
            pltpu.VMEM((8, 128), F32),
            pltpu.VMEM((8, 8, 128), F32),
            pltpu.VMEM((2, 8, 128), F32),
            pltpu.VMEM((16, 8, 128), F32),
            pltpu.VMEM((16, 8, 128), F32),
            pltpu.VMEM((16, 8, 128), F32),
        ]
        + [dma((len(GROUPS),))] * 2,
        compiler_params=pltpu.CompilerParams(
            collective_id=0, has_side_effects=True, vmem_limit_bytes=62 << 20
        ),
        name="cg2",
    )(probes, coords, features, noise_var, inv_scale, owner_map, block_pairs)
    return both[0], both[1]


def solution(mesh):
    return jax.shard_map(
        shards,
        mesh=mesh,
        in_specs=(
            P(("region", "dev"), None, None),
            P(("region", "dev"), None, None),
            P(("region", "dev"), None, None),
            P(("region", "dev"), None),
            P(),
            P("region", None),
            P("region", None, None),
        ),
        out_specs=(P(("region", "dev"), None, None), P(("region", "dev"), None, None)),
        check_vma=False,
    )
```
